128 devices in a mesh: ctx: 64 (over y_lo, z, x, core), ch: 2 (over y_hi).
Axes of the slice: x: 4, y: 4 (y_hi: 2, y_lo: 2; y = y_hi * 2 + y_lo), z: 4, core: 2. Of those that a mesh axis runs over, the one named last changes fastest.
Arguments:
- features: bfloat16 [3, 8192, 4096], P(None, 'ctx', 'ch'), may hold values from -6 to 6
- short_weight: float32 [3, 3, 4096], P(None, None, 'ch'), may hold values from -3 to 3
- skip: float32 [4096], P('ch'), may hold values from 0.5 to 1.5
- long_filter: float32 [8192, 256], P('ctx'), may hold values from -2 to 2
- cotangent: bfloat16 [8192, 4096], P('ctx', 'ch'), may hold values from -6 to 6
Outputs:
- mixed: bfloat16 [8192, 4096], P('ctx', 'ch')
- feature_gradient: float32 [3, 8192, 4096], P(None, 'ctx', 'ch')
- grad_short: float32 [3, 3, 4096], P(None, None, 'ch')
- grad_skip: float32 [4096], P('ch')
- grad_filter: float32 [8192, 256], P('ctx', 'ch')
The draws below stay inside these ranges and needn't reach their ends.
All inputs are finite; a program needn't handle non-finite values.
Results may differ from the reference program's by a relative error of at most 0.00105.
Values may be sent and summed in bfloat16 or wider, within the bound.
No kernel may reach another device: no remote copies, remote signals or barrier semaphores. Data moves between devices by JAX's collectives and lax.ppermute only.
A program may use at most 128 MiB of HBM per device.

```python
import math
import jax
import jax.numpy as jnp
from jax import lax

C = 4096
G = 256
TIMELINE_SPAN = 8192


def draw_long_filter(key, part):
    key = jax.random.fold_in(key, 7)
    lookup_entries = jax.random.split(key, 6)
    position = jnp.arange(TIMELINE_SPAN, dtype=jnp.float32)[:, None]
    slow_rate = jnp.exp(jax.random.uniform(lookup_entries[0], (G,), jnp.float32, math.log(0.3 / TIMELINE_SPAN), math.log(2.0 / TIMELINE_SPAN)))
    fast_rate = jax.random.uniform(lookup_entries[1], (G,), jnp.float32, 1.0 / 50.0, 1.0 / 30.0)
    fast = jax.random.randint(lookup_entries[2], (G,), 0, 10) < 5
    rate = jnp.where(fast, fast_rate, slow_rate)
    gathered_bundles = jax.random.randint(lookup_entries[3], (4,), 1, TIMELINE_SPAN)
    element_number = jnp.sum((jnp.arange(TIMELINE_SPAN)[:, None] >= gathered_bundles[None, :]).astype(jnp.float32), axis=1)[:, None]
    factor = jax.random.uniform(lookup_entries[4], (G,), jnp.float32, 0.5, 0.8)
    envelope = jnp.exp(-rate * position) * factor ** element_number * jnp.sqrt(1.0 - jnp.exp(-2.0 * rate))
    noise = jnp.clip(jax.random.normal(lookup_entries[5], (TIMELINE_SPAN, G), jnp.float32), -6.0, 6.0)
    return (noise * envelope).astype(jnp.float32)


def block_scale(stream_key, extent, pieces, least, high):
    factor_of = 1.0
    for dim, parts in pieces:
        draws = jax.random.uniform(jax.random.fold_in(jax.random.fold_in(stream_key, 6), dim), (parts,), jnp.float32, least / len(pieces), high / len(pieces))
        factor_of = factor_of * jnp.repeat(jnp.exp(draws), extent[dim] // parts).reshape((-1,) + (1,) * (len(extent) - 1 - dim))
    return factor_of


def bell_draw(rng, dims, scale, limit, pieces=(), kind=jnp.bfloat16):
    level = block_scale(rng, dims, pieces, -0.22, 0.18) if pieces else 1.0
    drawn = jax.random.normal(rng, dims, jnp.float32) * scale * level
    return jnp.minimum(jnp.maximum(drawn, -limit), limit).astype(kind)


def setup_inputs(seed: int = 0) -> dict:
    keys = jax.random.split(jax.random.key(seed), 6)
    features = bell_draw(keys[0], (3, TIMELINE_SPAN, C), 1.0, 6.0, ((1, 64), (2, 2)))
    short_weight = bell_draw(keys[1], (3, 3, C), 0.6, 3.0, ((2, 2),), jnp.float32)
    skip = jnp.clip(0.5 + 1.0 * jax.random.uniform(keys[2], (C,), jnp.float32) ** block_scale(keys[2], (C,), ((0, 2),), -0.2, 0.2), 0.5, 1.5)
    long_filter = draw_long_filter(jax.random.fold_in(keys[5], 71), 0)
    cotangent = bell_draw(keys[4], (TIMELINE_SPAN, C), 1.0, 6.0, ((0, 64), (1, 2)))
    return dict(features=features, short_weight=short_weight, skip=skip, long_filter=long_filter, cotangent=cotangent)


def causal_taps(signal, weight):
    padded = jnp.pad(signal, ((0, 0), (2, 0), (0, 0)))
    return weight[:, 0, None, :] * padded[:, 2:, :] + weight[:, 1, None, :] * padded[:, 1:-1, :] + weight[:, 2, None, :] * padded[:, :-2, :]

def reference(features, short_weight, skip, long_filter, cotangent):
    inputs = features.astype(jnp.float32)
    shaped = causal_taps(inputs, short_weight)
    query_f = shaped[0]
    key_f = shaped[1]
    value_f = shaped[2]
    mixer = key_f * value_f
    period = 2 * TIMELINE_SPAN
    mixer_spec = jnp.fft.rfft(mixer, n=period, axis=0)
    filter_spec = jnp.tile(jnp.fft.rfft(long_filter, n=period, axis=0), (1, C // G))
    convolved = jnp.fft.irfft(mixer_spec * filter_spec, n=period, axis=0)[:TIMELINE_SPAN] + skip * mixer
    mixed = (query_f * convolved).astype(jnp.bfloat16)
    upstream = cotangent.astype(jnp.float32)
    grad_query = upstream * convolved
    grad_conv = upstream * query_f
    conv_spec = jnp.fft.rfft(grad_conv, n=period, axis=0)
    grad_mixer = jnp.fft.irfft(conv_spec * jnp.conj(filter_spec), n=period, axis=0)[:TIMELINE_SPAN] + skip * grad_conv
    grad_shaped = jnp.stack([grad_query, grad_mixer * value_f, grad_mixer * key_f])
    padded_grad = jnp.pad(grad_shaped, ((0, 0), (0, 2), (0, 0)))
    feature_gradient = short_weight[:, 0, None, :] * padded_grad[:, :TIMELINE_SPAN, :] + short_weight[:, 1, None, :] * padded_grad[:, 1:TIMELINE_SPAN + 1, :] + short_weight[:, 2, None, :] * padded_grad[:, 2:, :]
    padded_in = jnp.pad(inputs, ((0, 0), (2, 0), (0, 0)))
    grad_short = jnp.stack([lax.optimization_barrier(jnp.sum(grad_shaped * padded_in[:, 2 - offset:2 - offset + TIMELINE_SPAN, :], axis=1)) for offset in range(3)], axis=1) / math.sqrt(TIMELINE_SPAN)
    grad_skip = lax.optimization_barrier(jnp.sum(grad_conv * mixer, axis=0)) / math.sqrt(TIMELINE_SPAN)
    cross = jnp.fft.irfft(conv_spec * jnp.conj(mixer_spec), n=period, axis=0)[:TIMELINE_SPAN]
    grad_filter = lax.optimization_barrier(jnp.sum(cross.reshape(TIMELINE_SPAN, C // G, G), axis=1)) / math.sqrt(TIMELINE_SPAN * (C // G))
    return (mixed, feature_gradient, grad_short, grad_skip, grad_filter)
```

```python
import functools
import math

import jax
import jax.numpy as jnp
import ml_dtypes
import numpy as np
from jax import lax
from jax.experimental import pallas as pl
from jax.experimental.pallas import tpu as pltpu
from jax.sharding import PartitionSpec as P

f32 = jnp.float32
bf16 = jnp.bfloat16

BLOCKS = 64
ROWS = 128
COPIES = 8
GROUPS = 256
OWN = GROUPS // BLOCKS
LINES = 72
PERIOD = 2 * BLOCKS * ROWS
SEND_ROWS = OWN * 4 * COPIES + 16
BACK_ROWS = OWN * 2 * COPIES + 16
LEVELS = 32000.0
BIAS = 124.0


def high_low(values):
    high = values.astype(ml_dtypes.bfloat16)
    low = (values - high.astype(np.float64)).astype(ml_dtypes.bfloat16)
    return high, low


def tables():
    k1 = np.arange(65)
    a = np.arange(BLOCKS)
    b = np.arange(ROWS)
    turn = 2.0 * np.pi * (k1[:, None] * a[None, :] % ROWS) / ROWS
    first = np.zeros((2 * LINES, BLOCKS))
    first[:65] = np.cos(turn)
    first[LINES : LINES + 65] = -np.sin(turn)
    weight = np.where((k1 == 0) | (k1 == 64), 1.0, 2.0)[:, None] / PERIOD
    last = np.zeros((BLOCKS, 2 * LINES))
    last[:, :65] = (weight * np.cos(turn)).T
    last[:, LINES : LINES + 65] = (-weight * np.sin(turn)).T
    twiddle = np.zeros((2, LINES, ROWS))
    twiddle[0, :65] = np.cos(2.0 * np.pi * k1[:, None] * b[None, :] / PERIOD)
    twiddle[1, :65] = np.sin(2.0 * np.pi * k1[:, None] * b[None, :] / PERIOD)
    angle = 2.0 * np.pi * (b[:, None] * b[None, :] % ROWS) / ROWS
    cosine, sine = np.cos(angle), np.sin(angle)
    forward = np.block([[cosine, -sine], [sine, cosine]])
    inverse = np.block([[cosine, sine], [-sine, cosine]])
    first_h, first_l = high_low(first)
    last_h, last_l = high_low(last)
    return (
        np.concatenate([first_h, first_h, first_l], axis=1),
        np.concatenate([last_h, last_h, last_l], axis=1),
        twiddle.astype(np.float32),
        np.stack(high_low(forward)),
        np.stack(high_low(inverse)),
    )


def split(values):
    high = values.astype(bf16)
    return high, (values - high.astype(f32)).astype(bf16)


def dot(left, right):
    return jnp.dot(left, right, preferred_element_type=f32)


def encode(values, scale):
    level = jnp.floor(jnp.abs(values) * (LEVELS / scale) + 0.5)
    step = jnp.floor(level * (1.0 / 128.0))
    part = 1.0 + (level - 128.0 * step) * (1.0 / 128.0)
    code = jnp.exp2(step - BIAS) * part
    return jnp.where(values < 0.0, -code, code).astype(bf16)


def decode(code, scale):
    size = jnp.abs(code)
    step = jnp.floor(jnp.log(size) * (1.0 / math.log(2.0)) + 0.002)
    level = 128.0 * (step + BIAS + (size * jnp.exp2(-step) - 1.0))
    value = level * (scale * (1.0 / LEVELS))
    return jnp.where(code < 0.0, -value, value)


def pack_kernel(feat_ref, cot_ref, filt_ref, out_ref, turned, taps):
    for part in range(4):
        source = cot_ref if part == 3 else feat_ref.at[part]
        for j in range(16):
            turned[part, 128 * j : 128 * (j + 1), :] = source[:, 128 * j : 128 * (j + 1)].astype(f32).T
    for j in range(2):
        rows = slice(128 * j, 128 * (j + 1))
        value = filt_ref[:, rows].T
        high = value.astype(bf16).astype(f32)
        rest = value - high
        middle = rest.astype(bf16).astype(f32)
        taps[0, rows, :] = high
        taps[1, rows, :] = middle
        taps[2, rows, :] = (rest - middle).astype(bf16).astype(f32)

    def one(d, _):
        for gi in range(OWN):
            g = OWN * d + gi
            tiles = [turned.at[part][pl.ds(g, COPIES, stride=GROUPS), :] for part in range(4)]
            out_ref[d, 32 * gi : 32 * gi + 16, :] = jnp.concatenate(tiles[:2], axis=0).astype(bf16)
            out_ref[d, 32 * gi + 16 : 32 * gi + 32, :] = jnp.concatenate(tiles[2:], axis=0).astype(bf16)
        pieces = [taps[part, pl.ds(OWN * d, OWN), :] for part in range(3)]
        pieces.append(jnp.zeros((OWN, ROWS), f32))
        out_ref[d, 128:144, :] = jnp.concatenate(pieces, axis=0).astype(bf16)
        return 0

    lax.fori_loop(0, BLOCKS, one, 0)


def conv_kernel(
    in_ref, weight_ref, first_ref, last_ref, twiddle_ref, forward_ref, inverse_ref,
    out_ref, left, right, spec_high, spec_low, lines, filt, cross, extra, taps,
):
    gi = pl.program_id(0)
    chunk = 8
    lane = lax.broadcasted_iota(jnp.int32, (1, 1, ROWS), 2)
    cosine, sine = twiddle_ref[0], twiddle_ref[1]

    def shaped_chunk(a0, carry):
        raw = in_ref[pl.ds(a0, chunk), pl.ds(pl.multiple_of(32 * gi, 32), 32), :].astype(f32)
        signal = raw[:, :24]
        one = pltpu.roll(signal, 1, 2)
        two = pltpu.roll(signal, 2, 2)
        one_before = jnp.concatenate([carry[0][None], one[:-1]], axis=0)
        two_before = jnp.concatenate([carry[1][None], two[:-1]], axis=0)
        shift_one = jnp.where(lane < 1, one_before, one)
        shift_two = jnp.where(lane < 2, two_before, two)
        weights = weight_ref[gi]
        shaped = []
        for i in range(3):
            rows = slice(8 * i, 8 * i + 8)
            shaped.append(
                weights[3 * i] * signal[:, rows]
                + weights[3 * i + 1] * shift_one[:, rows]
                + weights[3 * i + 2] * shift_two[:, rows]
            )
        return raw[:, 24:], (signal, shift_one, shift_two), shaped, (one[-1], two[-1])

    empty = (jnp.zeros((24, ROWS), f32), jnp.zeros((24, ROWS), f32))

    def shape_step(step, carry):
        a0 = chunk * step
        upstream, _, shaped, carry = shaped_chunk(a0, carry)
        rows = pl.ds(pl.multiple_of(COPIES * a0, 64), COPIES * chunk)
        left[rows, :] = (shaped[1] * shaped[2]).reshape(COPIES * chunk, ROWS)
        right[rows, :] = (upstream * shaped[0]).reshape(COPIES * chunk, ROWS)
        return carry

    lax.fori_loop(0, BLOCKS // chunk, shape_step, empty)

    def pick(ref, k):
        return ref[pl.ds(k, BLOCKS, stride=COPIES), :]

    def to_lines(blocks, base):
        both = jnp.concatenate(blocks, axis=1)
        high, low = split(both)
        mid = dot(first_ref[...], jnp.concatenate([high, low, high], axis=0))
        out = []
        for j in range(2):
            real = mid[:LINES, ROWS * j : ROWS * (j + 1)]
            imag = mid[LINES:, ROWS * j : ROWS * (j + 1)]
            out.append(jnp.concatenate([real * cosine + imag * sine, imag * cosine - real * sine], axis=1))
        keep(jnp.concatenate(out, axis=0), base)

    def keep(values, base):
        high, low = split(values)
        spec_high[base : base + 2 * LINES, :] = high
        spec_low[base : base + 2 * LINES, :] = low

    def over_rows(matrix, count):
        high = spec_high[: LINES * count, :]
        return dot(high, matrix[0]) + dot(spec_low[: LINES * count, :], matrix[0]) + dot(high, matrix[1])

    def from_lines(values):
        pieces = []
        for j in range(2):
            real = values[LINES * j : LINES * (j + 1), :ROWS]
            imag = values[LINES * j : LINES * (j + 1), ROWS:]
            pieces.append(jnp.concatenate([real * cosine - imag * sine, imag * cosine + real * sine], axis=0))
        high, low = split(jnp.concatenate(pieces, axis=1))
        both = dot(last_ref[...], jnp.concatenate([high, low, high], axis=0))
        return both[:, :ROWS], both[:, ROWS:]

    @pl.when(gi == 0)
    def _():
        def widen(a, _):
            taps[pl.ds(pl.multiple_of(16 * a, 16), 16), :] = in_ref[a, 128:144, :].astype(f32)
            return 0

        lax.fori_loop(0, BLOCKS, widen, 0)
        blocks = []
        for f in range(OWN):
            parts = [taps[pl.ds(OWN * part + f, BLOCKS, stride=16), :] for part in range(3)]
            blocks.append(parts[0] + parts[1] + parts[2])
        for pair in range(OWN // 2):
            to_lines(blocks[2 * pair : 2 * pair + 2], 2 * LINES * pair)
        filt[...] = over_rows(forward_ref, OWN).reshape(OWN, LINES, 2 * ROWS)
        extra[...] = jnp.zeros_like(extra)

    for pair in range(COPIES // 2):
        to_lines([pick(left, 2 * pair), pick(left, 2 * pair + 1)], 2 * LINES * pair)
    for pair in range(COPIES // 2):
        to_lines([pick(right, 2 * pair), pick(right, 2 * pair + 1)], 2 * LINES * (COPIES // 2 + pair))
    lines[...] = over_rows(forward_ref, 2 * COPIES)

    filt_real, filt_imag = filt[gi, :, :ROWS], filt[gi, :, ROWS:]
    cross_real = jnp.zeros((LINES, ROWS), f32)
    cross_imag = jnp.zeros((LINES, ROWS), f32)
    for pair in range(COPIES // 2):
        forth, back = [], []
        for k in (2 * pair, 2 * pair + 1):
            here = slice(LINES * k, LINES * (k + 1))
            there = slice(LINES * (COPIES + k), LINES * (COPIES + k + 1))
            mix_real, mix_imag = lines[here, :ROWS], lines[here, ROWS:]
            grad_real, grad_imag = lines[there, :ROWS], lines[there, ROWS:]
            forth.append(
                jnp.concatenate(
                    [mix_real * filt_real - mix_imag * filt_imag, mix_real * filt_imag + mix_imag * filt_real], axis=1
                )
            )
            back.append(
                jnp.concatenate(
                    [
                        grad_real * filt_real + grad_imag * filt_imag,
                        grad_imag * filt_real - grad_real * filt_imag,
                    ],
                    axis=1,
                )
            )
            cross_real = cross_real + grad_real * mix_real + grad_imag * mix_imag
            cross_imag = cross_imag + grad_imag * mix_real - grad_real * mix_imag
        keep(jnp.concatenate(forth, axis=0), 2 * LINES * pair)
        keep(jnp.concatenate(back, axis=0), 2 * LINES * (COPIES // 2 + pair))
    cross[gi] = jnp.concatenate([cross_real, cross_imag], axis=1)
    lines[...] = over_rows(inverse_ref, 2 * COPIES)

    skip = weight_ref[gi, 9]
    for target, base in ((left, 0), (right, COPIES)):
        for pair in range(COPIES // 2):
            k = 2 * pair
            low, high = from_lines(lines[LINES * (base + k) : LINES * (base + k + 2), :])
            for j, value in ((0, low), (1, high)):
                place = pl.ds(k + j, BLOCKS, stride=COPIES)
                target[place, :] = value

    def finish(step, state):
        carry, sums = state
        a0 = chunk * step
        upstream, shifts, shaped, carry = shaped_chunk(a0, carry)
        rows = pl.ds(pl.multiple_of(COPIES * a0, 64), COPIES * chunk)
        mixer = shaped[1] * shaped[2]
        grad_conv = upstream * shaped[0]
        conv = left[rows, :].reshape(chunk, COPIES, ROWS) + skip * mixer
        grad_mixer = right[rows, :].reshape(chunk, COPIES, ROWS) + skip * grad_conv
        left[rows, :] = conv.reshape(COPIES * chunk, ROWS)
        right[rows, :] = grad_mixer.reshape(COPIES * chunk, ROWS)
        grads = (upstream * conv, grad_mixer * shaped[2], grad_mixer * shaped[1])
        new = []
        for i in range(3):
            for j in range(3):
                new.append(sums[3 * i + j] + jnp.sum(grads[i] * shifts[j][:, 8 * i : 8 * i + 8], axis=0))
        new.append(sums[9] + jnp.sum(grad_conv * mixer, axis=0))
        return carry, tuple(new)

    zero = jnp.zeros((COPIES, ROWS), f32)
    _, sums = lax.fori_loop(0, BLOCKS // chunk, finish, (empty, (zero,) * 10))

    flat = lane[0]
    totals = zero
    for i in range(10):
        total = jnp.sum(sums[i], axis=1, keepdims=True) * (1.0 / math.sqrt(BLOCKS * ROWS))
        totals = totals + jnp.where(flat == 16 + i, total, 0.0)

    def send(step, _):
        a0 = chunk * step
        rows = pl.ds(pl.multiple_of(COPIES * a0, 64), COPIES * chunk)
        after = pl.ds(pl.multiple_of(jnp.minimum(COPIES * (a0 + chunk), COPIES * (BLOCKS - 1)), COPIES), COPIES)
        keep_last = jnp.where(a0 + chunk < BLOCKS, 1.0, 0.0)
        codes = []
        entry = jnp.broadcast_to(totals, (chunk, COPIES, ROWS))
        for slot, ref in ((0, left), (1, right)):
            value = ref[rows, :].reshape(chunk, COPIES, ROWS)
            largest = jnp.max(jnp.abs(value), axis=2, keepdims=True)
            scale = (jnp.maximum(largest, 1e-30) * (1.0 + 1.0 / 128.0)).astype(bf16).astype(f32)
            codes.append(encode(value, scale))
            following = jnp.concatenate([value[1:], ref[after, :][None] * keep_last], axis=0)
            entry = entry + jnp.where(lane == 26 + slot, scale, 0.0)
            moved = pltpu.roll(following, 28 + 2 * slot, 2)
            entry = entry + jnp.where((lane >= 28 + 2 * slot) & (lane < 30 + 2 * slot), moved, 0.0)
        out_ref[pl.ds(a0, chunk), pl.ds(pl.multiple_of(16 * gi, 16), 16), :] = jnp.concatenate(codes, axis=1)
        extra[rows, :] = extra[rows, :] + pltpu.roll(entry, 32 * gi, 2).reshape(COPIES * chunk, ROWS)
        return 0

    lax.fori_loop(0, BLOCKS // chunk, send, 0)

    @pl.when(gi == OWN - 1)
    def _():
        for pair in range(OWN // 2):
            keep(cross[2 * pair : 2 * pair + 2].reshape(2 * LINES, 2 * ROWS), 2 * LINES * pair)
        temporal = over_rows(inverse_ref, OWN)
        scale = 1.0 / math.sqrt(BLOCKS * ROWS * 2 * COPIES)
        for pair in range(OWN // 2):
            both = from_lines(temporal[2 * LINES * pair : 2 * LINES * (pair + 1)])
            for j in range(2):
                f = 2 * pair + j
                value = both[j] * scale
                for k in range(COPIES):
                    place = pl.ds(k, BLOCKS, stride=COPIES)
                    moved = pltpu.roll(value, (32 * f - 16 * k) % ROWS, 1)
                    inside = (flat >= 32 * f) & (flat < 32 * f + 16)
                    extra[place, :] = jnp.where(inside, moved, extra[place, :])

        def write(a, _):
            value = extra[pl.ds(pl.multiple_of(COPIES * a, COPIES), COPIES), :]
            high = value.astype(bf16).astype(f32)
            out_ref[a, 64:80, :] = jnp.concatenate([high, value - high], axis=0).astype(bf16)
            return 0

        lax.fori_loop(0, BLOCKS, write, 0)


def extras_kernel(in_ref, spread_ref, filt_ref, ext_ref, wide):
    def widen(d, _):
        wide[pl.ds(pl.multiple_of(16 * d, 16), 16), :] = in_ref[d, :, :].astype(f32)
        return 0

    lax.fori_loop(0, BLOCKS, widen, 0)
    for k in range(COPIES):
        both = []
        for part in range(2):
            piece = wide[pl.ds(8 * part + k, BLOCKS, stride=16), :]
            both.append(piece.T.astype(bf16))
        total = jnp.zeros((32, GROUPS), f32)
        for gi in range(OWN):
            rows = slice(32 * gi, 32 * gi + 32)
            for part in range(2):
                total = total + dot(both[part][rows], spread_ref[gi])
        filt_ref[16 * k : 16 * (k + 1), :] = total[:16]
        ext_ref[:, GROUPS * k : GROUPS * (k + 1)] = total[16:]


def finish_kernel(
    in_ref, feat_ref, cot_ref, before_ref, after_ref, weight_ref, ext_ref, mixed_ref, grad_ref, wide
):
    k = pl.program_id(0)

    @pl.when(k == 0)
    def _():
        def widen(d, _):
            wide[pl.ds(pl.multiple_of(64 * d, 64), 64), :] = in_ref[d, :64, :].astype(f32)
            return 0

        lax.fori_loop(0, BLOCKS, widen, 0)

    row = lax.broadcasted_iota(jnp.int32, (ROWS, 1), 0)
    signals = []
    for slot in range(2):
        halves = []
        for half in range(2):
            place = pl.ds(2048 * half + 8 * slot + k, 128, stride=16)
            halves.append(wide[place, :].T)
        signals.append(decode(jnp.concatenate(halves, axis=1), ext_ref[10 + slot : 11 + slot, :]))
    conv, grad_mixer = signals
    upstream = cot_ref[...].astype(f32)
    shaped, shaped_after, weights = [], [], []
    for i in range(3):
        taps = [weight_ref[3 * i + j : 3 * i + j + 1, :] for j in range(3)]
        weights.append(taps)
        value = feat_ref[i].astype(f32)
        before = before_ref[i].astype(f32)
        after = after_ref[i].astype(f32)
        one = jnp.where(row == 0, before[1:2], pltpu.roll(value, 1, 0))
        two = jnp.where(row == 0, before[0:1], jnp.where(row == 1, before[1:2], pltpu.roll(value, 2, 0)))
        shaped.append(taps[0] * value + taps[1] * one + taps[2] * two)
        final, second = value[ROWS - 1 : ROWS], value[ROWS - 2 : ROWS - 1]
        shaped_after.append(
            (
                taps[0] * after[0:1] + taps[1] * final + taps[2] * second,
                taps[0] * after[1:2] + taps[1] * after[0:1] + taps[2] * final,
            )
        )
    mixed_ref[...] = (shaped[0] * conv).astype(bf16)
    grads = (upstream * conv, grad_mixer * shaped[2], grad_mixer * shaped[1])
    upstream_after = after_ref[0].astype(f32)
    for i in range(3):
        grad = grads[i]
        following = []
        for t in range(2):
            conv_t = ext_ref[12 + t : 13 + t, :]
            mixer_t = ext_ref[14 + t : 15 + t, :]
            if i == 0:
                following.append(upstream_after[t : t + 1] * conv_t)
            else:
                following.append(mixer_t * shaped_after[3 - i][t])
        one = jnp.where(row == ROWS - 1, following[0], pltpu.roll(grad, ROWS - 1, 0))
        two = jnp.where(
            row == ROWS - 1,
            following[1],
            jnp.where(row == ROWS - 2, following[0], pltpu.roll(grad, ROWS - 2, 0)),
        )
        grad_ref[i] = weights[i][0] * grad + weights[i][1] * one + weights[i][2] * two


def exchange(values):
    return lax.all_to_all(values, "ctx", split_axis=0, concat_axis=0, tiled=True)


def shift(block, distance):
    route = [(i, i + distance) for i in range(BLOCKS) if 0 <= i + distance < BLOCKS]
    return lax.ppermute(block, "ctx", route)


def shards(features, short_weight, skip, long_filter, cotangent):
    rank = lax.axis_index("ctx")
    half = lax.axis_index("ch")
    breadth = features.shape[2]
    limit = pltpu.CompilerParams(vmem_limit_bytes=56 * 2**20)

    packed = pl.pallas_call(
        pack_kernel,
        out_shape=jax.ShapeDtypeStruct((BLOCKS, SEND_ROWS, ROWS), bf16),
        scratch_shapes=[pltpu.VMEM((4, breadth, ROWS), f32), pltpu.VMEM((3, GROUPS, ROWS), f32)],
        compiler_params=limit,
        name="pack",
    )(features, cotangent, long_filter)

    before = shift(features[:, ROWS - 2 :, :], 1)
    after = shift(jnp.concatenate([cotangent[None, :2], features[1:, :2]], axis=0), -1)

    first, last, twiddle, forward, inverse = tables()
    weights = jnp.concatenate([short_weight.reshape(9, breadth), skip[None]], axis=0)
    own = lax.dynamic_index_in_dim(weights.reshape(10, COPIES, BLOCKS, OWN), rank, 2, keepdims=False)
    own = jnp.broadcast_to(jnp.transpose(own, (2, 0, 1))[..., None], (OWN, 10, COPIES, ROWS))

    gathered = exchange(packed)

    vmem = pl.BlockSpec(memory_space=pltpu.VMEM)
    returned = pl.pallas_call(
        conv_kernel,
        grid=(OWN,),
        in_specs=[vmem] * 7,
        out_specs=vmem,
        out_shape=jax.ShapeDtypeStruct((BLOCKS, BACK_ROWS, ROWS), bf16),
        scratch_shapes=[
            pltpu.VMEM((COPIES * BLOCKS, ROWS), f32),
            pltpu.VMEM((COPIES * BLOCKS, ROWS), f32),
            pltpu.VMEM((2 * COPIES * LINES, 2 * ROWS), bf16),
            pltpu.VMEM((2 * COPIES * LINES, 2 * ROWS), bf16),
            pltpu.VMEM((2 * COPIES * LINES, 2 * ROWS), f32),
            pltpu.VMEM((OWN, LINES, 2 * ROWS), f32),
            pltpu.VMEM((OWN, LINES, 2 * ROWS), f32),
            pltpu.VMEM((COPIES * BLOCKS, ROWS), f32),
            pltpu.VMEM((16 * BLOCKS, ROWS), f32),
        ],
        compiler_params=limit,
        name="conv",
    )(gathered, own, first, last, twiddle, forward, inverse)

    home = exchange(returned)

    spread = np.zeros((OWN, BLOCKS, GROUPS), ml_dtypes.bfloat16)
    for gi in range(OWN):
        spread[gi, np.arange(BLOCKS), OWN * np.arange(BLOCKS) + gi] = 1.0
    raw_filter, ext = pl.pallas_call(
        extras_kernel,
        grid=(1,),
        in_specs=[
            pl.BlockSpec((BLOCKS, 16, ROWS), lambda i: (0, 4, 0)),
            pl.BlockSpec((OWN, BLOCKS, GROUPS), lambda i: (0, 0, 0)),
        ],
        out_specs=[
            pl.BlockSpec((ROWS, GROUPS), lambda i: (0, 0)),
            pl.BlockSpec((16, breadth), lambda i: (0, 0)),
        ],
        out_shape=[
            jax.ShapeDtypeStruct((ROWS, GROUPS), f32),
            jax.ShapeDtypeStruct((16, breadth), f32),
        ],
        scratch_shapes=[pltpu.VMEM((16 * BLOCKS, ROWS), f32)],
        compiler_params=limit,
        name="extras",
    )(home, spread)

    mine = lax.dynamic_slice_in_dim(raw_filter, half * (GROUPS // 2), GROUPS // 2, axis=1)
    other = lax.dynamic_slice_in_dim(raw_filter, (1 - half) * (GROUPS // 2), GROUPS // 2, axis=1)
    arrived = lax.ppermute(other, "ch", [(0, 1), (1, 0)])

    mixed, feature_gradient = pl.pallas_call(
        finish_kernel,
        grid=(COPIES,),
        in_specs=[
            pl.BlockSpec((BLOCKS, BACK_ROWS, ROWS), lambda k: (0, 0, 0)),
            pl.BlockSpec((3, ROWS, GROUPS), lambda k: (0, 0, k)),
            pl.BlockSpec((ROWS, GROUPS), lambda k: (0, k)),
            pl.BlockSpec((3, 2, GROUPS), lambda k: (0, 0, k)),
            pl.BlockSpec((3, 2, GROUPS), lambda k: (0, 0, k)),
            pl.BlockSpec((9, GROUPS), lambda k: (0, k)),
            pl.BlockSpec((16, GROUPS), lambda k: (0, k)),
        ],
        out_specs=[
            pl.BlockSpec((ROWS, GROUPS), lambda k: (0, k)),
            pl.BlockSpec((3, ROWS, GROUPS), lambda k: (0, 0, k)),
        ],
        out_shape=[
            jax.ShapeDtypeStruct((ROWS, breadth), bf16),
            jax.ShapeDtypeStruct((3, ROWS, breadth), f32),
        ],
        scratch_shapes=[pltpu.VMEM((64 * BLOCKS, ROWS), f32)],
        compiler_params=limit,
        name="finish",
    )(home, features, cotangent, before, after, short_weight.reshape(9, breadth), ext)

    grad_short = ext[:9].reshape(3, 3, breadth)
    grad_skip = ext[9]
    return (mixed, feature_gradient, grad_short, grad_skip, mine + arrived)


def solution(mesh):
    return jax.shard_map(
        shards,
        mesh=mesh,
        in_specs=(
            P(None, "ctx", "ch"),
            P(None, None, "ch"),
            P("ch"),
            P("ctx", None),
            P("ctx", "ch"),
        ),
        out_specs=(
            P("ctx", "ch"),
            P(None, "ctx", "ch"),
            P(None, None, "ch"),
            P("ch"),
            P("ctx", "ch"),
        ),
        check_vma=False,
    )
```

```python
import functools
import math

import jax
import jax.numpy as jnp
import ml_dtypes
import numpy as np
from jax import lax
from jax.experimental import pallas as pl
from jax.experimental.pallas import tpu as pltpu
from jax.sharding import PartitionSpec as P

f32 = jnp.float32
bf16 = jnp.bfloat16

BLOCKS = 64
ROWS = 128
COPIES = 8
GROUPS = 256
OWN = GROUPS // BLOCKS
LINES = 72
PERIOD = 2 * BLOCKS * ROWS
SIGNAL_ROWS = OWN * 4 * COPIES
SEND_ROWS = SIGNAL_ROWS + 2 * OWN
RESULT_ROWS = OWN * 2 * COPIES
BACK_ROWS = RESULT_ROWS + 2 * COPIES
AFTER, SCALE, TOTAL, FILTER = 0, 4, 6, 16
LEVELS = 32000.0
BIAS = 124.0
GANG = 8
SPACING = GROUPS + 1
LIMIT = pltpu.CompilerParams(vmem_limit_bytes=56 * 2**20)


def high_low(values):
    high = values.astype(ml_dtypes.bfloat16)
    low = (values - high.astype(np.float64)).astype(ml_dtypes.bfloat16)
    return high, low


def tables():
    k1 = np.arange(65)
    a = np.arange(BLOCKS)
    b = np.arange(ROWS)
    turn = 2.0 * np.pi * (k1[:, None] * a[None, :] % ROWS) / ROWS
    first = np.zeros((2 * LINES, BLOCKS))
    first[:65] = np.cos(turn)
    first[LINES : LINES + 65] = -np.sin(turn)
    weight = np.where((k1 == 0) | (k1 == 64), 1.0, 2.0)[:, None] / PERIOD
    last = np.zeros((BLOCKS, 2 * LINES))
    last[:, :65] = (weight * np.cos(turn)).T
    last[:, LINES : LINES + 65] = (-weight * np.sin(turn)).T
    twiddle = np.zeros((2, LINES, ROWS))
    twiddle[0, :65] = np.cos(2.0 * np.pi * k1[:, None] * b[None, :] / PERIOD)
    twiddle[1, :65] = np.sin(2.0 * np.pi * k1[:, None] * b[None, :] / PERIOD)
    angle = 2.0 * np.pi * (b[:, None] * b[None, :] % ROWS) / ROWS
    cosine, sine = np.cos(angle), np.sin(angle)
    forward = np.block([[cosine, -sine], [sine, cosine]])
    inverse = np.block([[cosine, sine], [-sine, cosine]])
    first_h, first_l = high_low(first)
    last_h, last_l = high_low(last)
    forward_h, forward_l = high_low(forward)
    inverse_h, inverse_l = high_low(inverse)
    return (
        np.concatenate([first_h, first_h, first_l], axis=1),
        np.concatenate([last_h, last_h, last_l], axis=1),
        twiddle.astype(np.float32),
        np.concatenate([forward_h, forward_h, forward_l], axis=0),
        np.concatenate([inverse_h, inverse_h, inverse_l], axis=0),
    )


def split(values):
    high = values.astype(bf16)
    return high, (values - high.astype(f32)).astype(bf16)


def dot(left, right):
    return jnp.dot(left, right, preferred_element_type=f32)


def encode(values, scale):
    level = jnp.floor(jnp.abs(values) * (LEVELS / scale) + 0.5)
    step = jnp.floor(level * (1.0 / 128.0))
    part = 1.0 + (level - 128.0 * step) * (1.0 / 128.0)
    code = jnp.exp2(step - BIAS) * part
    return jnp.where(values < 0.0, -code, code).astype(bf16)


def decode(code, scale):
    size = jnp.abs(code)
    step = jnp.floor(jnp.log(size) * (1.0 / math.log(2.0)) + 0.002)
    level = 128.0 * (step + BIAS + (size * jnp.exp2(-step) - 1.0))
    value = level * (scale * (1.0 / LEVELS))
    return jnp.where(code < 0.0, -value, value)


def pack_kernel(
    feat_ref, cot_ref, filt_ref, out_ref, feat, cot, filt, packed, turned, taps, feat_sem, cot_sem, filt_sem, out_sem
):
    arriving = []
    for k in range(COPIES):
        lanes = pl.ds(GROUPS * k, GROUPS)
        arriving.append(
            (
                pltpu.make_async_copy(feat_ref.at[:, :, lanes], feat.at[k], feat_sem.at[k]),
                pltpu.make_async_copy(cot_ref.at[:, lanes], cot.at[k], cot_sem.at[k]),
            )
        )
    filter_copy = pltpu.make_async_copy(filt_ref, filt, filt_sem)
    filter_copy.start()
    for copies in arriving:
        for copy in copies:
            copy.start()

    filter_copy.wait()
    value = filt[...].T
    high = value.astype(bf16).astype(f32)
    taps[0] = high
    taps[1] = value - high
    for k in range(COPIES):
        for copy in arriving[k]:
            copy.wait()
        for part in range(4):
            source = cot[k] if part == 3 else feat[k, part]
            turned[part, SPACING * k : SPACING * k + GROUPS, :] = source.astype(f32).T

    def one(d, _):
        for gi in range(OWN):
            n = OWN * d + gi
            tiles = [turned.at[part][pl.ds(n, COPIES, stride=SPACING), :] for part in range(4)]
            packed[d, 32 * gi : 32 * gi + 16, :] = jnp.concatenate(tiles[:2], axis=0).astype(bf16)
            packed[d, 32 * gi + 16 : 32 * gi + 32, :] = jnp.concatenate(tiles[2:], axis=0).astype(bf16)
        pieces = [taps[part, pl.ds(OWN * d, OWN), :] for part in range(2)]
        packed[d, SIGNAL_ROWS:SEND_ROWS, :] = jnp.concatenate(pieces, axis=0).astype(bf16)
        return 0

    leaving = []
    share = BLOCKS // 4
    for j in range(4):
        lax.fori_loop(share * j, share * (j + 1), one, 0, unroll=4)
        place = pl.ds(share * j, share)
        leaving.append(pltpu.make_async_copy(packed.at[place], out_ref.at[place], out_sem.at[j]))
        leaving[-1].start()
    for copy in leaving:
        copy.wait()


def conv_kernel(
    in_ref, taps_ref, weight_ref, first_ref, last_ref, twiddle_ref, forward_ref, inverse_ref, out_ref,
    raw_buf, code_buf, in_sem, out_sem,
    left, right, shift_one, shift_two, spec_high, spec_low, lines, filt, cross, extra, taps, totals, own,
):
    chunk = 8
    steps = BLOCKS // chunk
    lane = lax.broadcasted_iota(jnp.int32, (1, 1, ROWS), 2)
    flat = lane[0]
    cosine, sine = twiddle_ref[0], twiddle_ref[1]

    def arriving(gi):
        rows = pl.ds(pl.multiple_of(4 * COPIES * gi, 4 * COPIES), 4 * COPIES)
        return pltpu.make_async_copy(in_ref.at[:, rows, :], raw_buf.at[gi], in_sem.at[gi])

    def leaving(gi):
        rows = pl.ds(pl.multiple_of(2 * COPIES * gi, 2 * COPIES), 2 * COPIES)
        return pltpu.make_async_copy(code_buf.at[gi], out_ref.at[:, rows, :], out_sem.at[gi])

    for gi in range(OWN):
        arriving(gi).start()

    def tile_rows(a0):
        return pl.ds(pl.multiple_of(COPIES * a0, 64), COPIES * chunk)

    def raw_chunk(gi, a0):
        return raw_buf[gi, pl.ds(a0, chunk)].astype(f32)

    def shape(weights, signals):
        shaped = []
        for i in range(3):
            rows = slice(8 * i, 8 * i + 8)
            shaped.append(sum(weights[3 * i + j] * signals[j][:, rows] for j in range(3)))
        return shaped

    def pick(ref, k):
        return ref[pl.ds(k, BLOCKS, stride=COPIES), :]

    def to_lines(blocks, base):
        both = jnp.concatenate(blocks, axis=1)
        high, low = split(both)
        mid = dot(first_ref[...], jnp.concatenate([high, low, high], axis=0))
        out = []
        for j in range(2):
            real = mid[:LINES, ROWS * j : ROWS * (j + 1)]
            imag = mid[LINES:, ROWS * j : ROWS * (j + 1)]
            out.append(jnp.concatenate([real * cosine + imag * sine, imag * cosine - real * sine], axis=1))
        keep(jnp.concatenate(out, axis=0), base)

    def keep(values, base):
        high, low = split(values)
        spec_high[base : base + 2 * LINES, :] = high
        spec_low[base : base + 2 * LINES, :] = low

    def over_rows(matrix, begin, count):
        rows = slice(LINES * begin, LINES * (begin + count))
        high = spec_high[rows, :]
        return dot(jnp.concatenate([high, spec_low[rows, :], high], axis=1), matrix[...])

    def from_lines(values):
        pieces = []
        for j in range(2):
            real = values[LINES * j : LINES * (j + 1), :ROWS]
            imag = values[LINES * j : LINES * (j + 1), ROWS:]
            pieces.append(jnp.concatenate([real * cosine - imag * sine, imag * cosine + real * sine], axis=0))
        high, low = split(jnp.concatenate(pieces, axis=1))
        both = dot(last_ref[...], jnp.concatenate([high, low, high], axis=0))
        return both[:, :ROWS], both[:, ROWS:]

    def main(gi, _):
        weights = [weight_ref[gi, i] for i in range(10)]
        arriving(gi).wait()

        def shape_step(step, carry):
            a0 = chunk * step
            raw = raw_chunk(gi, a0)
            signal = raw[:, :24]
            one = pltpu.roll(signal, 1, 2)
            two = pltpu.roll(signal, 2, 2)
            one_before = jnp.concatenate([carry[0][None], one[:-1]], axis=0)
            two_before = jnp.concatenate([carry[1][None], two[:-1]], axis=0)
            delayed = (jnp.where(lane < 1, one_before, one), jnp.where(lane < 2, two_before, two))
            shift_one[pl.ds(a0, chunk)] = delayed[0]
            shift_two[pl.ds(a0, chunk)] = delayed[1]
            shaped = shape(weights, (signal,) + delayed)
            left[tile_rows(a0), :] = (shaped[1] * shaped[2]).reshape(COPIES * chunk, ROWS)
            right[tile_rows(a0), :] = (raw[:, 24:] * shaped[0]).reshape(COPIES * chunk, ROWS)
            return one[-1], two[-1]

        empty = jnp.zeros((24, ROWS), f32)
        lax.fori_loop(0, steps, shape_step, (empty, empty), unroll=8)

        for base, ref in ((0, left), (COPIES, right)):
            for k in range(0, COPIES, GANG):
                for j in range(k, k + GANG, 2):
                    to_lines([pick(ref, j), pick(ref, j + 1)], LINES * (base + j))
                lines[LINES * (base + k) : LINES * (base + k + GANG), :] = over_rows(forward_ref, base + k, GANG)

        filt_real, filt_imag = filt[gi, :, :ROWS], filt[gi, :, ROWS:]
        cross_real = jnp.zeros((LINES, ROWS), f32)
        cross_imag = jnp.zeros((LINES, ROWS), f32)
        for pair in range(COPIES // 2):
            forth, back = [], []
            for k in (2 * pair, 2 * pair + 1):
                here = slice(LINES * k, LINES * (k + 1))
                there = slice(LINES * (COPIES + k), LINES * (COPIES + k + 1))
                mix_real, mix_imag = lines[here, :ROWS], lines[here, ROWS:]
                grad_real, grad_imag = lines[there, :ROWS], lines[there, ROWS:]
                forth.append(
                    jnp.concatenate(
                        [mix_real * filt_real - mix_imag * filt_imag, mix_real * filt_imag + mix_imag * filt_real], axis=1
                    )
                )
                back.append(
                    jnp.concatenate(
                        [
                            grad_real * filt_real + grad_imag * filt_imag,
                            grad_imag * filt_real - grad_real * filt_imag,
                        ],
                        axis=1,
                    )
                )
                cross_real = cross_real + grad_real * mix_real + grad_imag * mix_imag
                cross_imag = cross_imag + grad_imag * mix_real - grad_real * mix_imag
            keep(jnp.concatenate(forth, axis=0), 2 * LINES * pair)
            keep(jnp.concatenate(back, axis=0), 2 * LINES * (COPIES // 2 + pair))
        cross[gi] = jnp.concatenate([cross_real, cross_imag], axis=1)
        for k in range(0, COPIES, GANG):
            for target, base in ((left, 0), (right, COPIES)):
                values = over_rows(inverse_ref, base + k, GANG)
                for j in range(0, GANG, 2):
                    pair = from_lines(values[LINES * j : LINES * (j + 2), :])
                    for i in range(2):
                        target[pl.ds(k + j + i, BLOCKS, stride=COPIES), :] = pair[i]

        def finish(step, sums):
            a0 = chunk * step
            rows = tile_rows(a0)
            raw = raw_chunk(gi, a0)
            upstream = raw[:, 24:]
            signals = (raw[:, :24], shift_one[pl.ds(a0, chunk)], shift_two[pl.ds(a0, chunk)])
            shaped = shape(weights, signals)
            mixer = shaped[1] * shaped[2]
            grad_conv = upstream * shaped[0]
            conv = left[rows, :].reshape(chunk, COPIES, ROWS) + weights[9] * mixer
            grad_mixer = right[rows, :].reshape(chunk, COPIES, ROWS) + weights[9] * grad_conv
            grads = (upstream * conv, grad_mixer * shaped[2], grad_mixer * shaped[1])
            new = []
            for i in range(3):
                for j in range(3):
                    new.append(sums[3 * i + j] + jnp.sum(grads[i] * signals[j][:, 8 * i : 8 * i + 8], axis=0))
            new.append(sums[9] + jnp.sum(grad_conv * mixer, axis=0))

            codes = []
            entry = jnp.zeros((COPIES, ROWS), f32)
            for slot, value in ((0, conv), (1, grad_mixer)):
                largest = jnp.max(jnp.max(jnp.abs(value), axis=0), axis=1, keepdims=True)
                scale = (jnp.maximum(largest, 1e-30) * (1.0 + 1.0 / 128.0)).astype(bf16).astype(f32)
                codes.append(encode(value, scale))
                entry = entry + jnp.where(flat == SCALE + slot, scale, 0.0)
            code_buf[gi, pl.ds(a0, chunk)] = jnp.concatenate(codes, axis=1)
            ahead = jnp.where(lane < 2, conv, jnp.where(lane < 4, pltpu.roll(grad_mixer, 2, 2), 0.0))
            ahead = pltpu.roll(ahead, 32 * gi, 2)
            extra[pl.ds(a0, chunk)] = extra[pl.ds(a0, chunk)] + ahead
            entry = pltpu.roll(entry, 32 * gi, 1)
            extra[pl.ds(a0 + 1, chunk)] = extra[pl.ds(a0 + 1, chunk)] + entry[None]
            return tuple(new)

        zero = jnp.zeros((COPIES, ROWS), f32)
        sums = lax.fori_loop(0, steps, finish, (zero,) * 10, unroll=8)

        total = zero
        for i in range(10):
            value = jnp.sum(sums[i], axis=1, keepdims=True) * (1.0 / math.sqrt(BLOCKS * ROWS))
            total = total + jnp.where(flat == TOTAL + i, value, 0.0)
        totals[gi] = pltpu.roll(total, 32 * gi, 1)
        leaving(gi).start()
        return 0

    def wrap_up():
        for f in range(0, OWN, 2):
            keep(cross[f : f + 2].reshape(2 * LINES, 2 * ROWS), LINES * f)
        temporal = over_rows(inverse_ref, 0, OWN)
        scale = 1.0 / math.sqrt(BLOCKS * ROWS * 2 * COPIES)
        for f in range(0, OWN, 2):
            both = from_lines(temporal[LINES * f : LINES * (f + 2)])
            for j in range(2):
                value = both[j] * scale
                for k in range(COPIES):
                    moved = pltpu.roll(value, (32 * (f + j) + FILTER - 16 * k) % ROWS, 1)
                    own.at[f + j][pl.ds(k, BLOCKS, stride=COPIES), :] = moved
        every = totals[0] + totals[1] + totals[2] + totals[3]

        def write(step, _):
            a0 = chunk * step
            value = extra[pl.ds(a0 + 1, chunk)] + every[None]
            for f in range(OWN):
                inside = (lane >= 32 * f + FILTER) & (lane < 32 * f + 32)
                value = jnp.where(inside, own[f, tile_rows(a0), :].reshape(chunk, COPIES, ROWS), value)
            high = value.astype(bf16).astype(f32)
            code_buf[OWN, pl.ds(a0, chunk)] = jnp.concatenate([high, value - high], axis=1).astype(bf16)
            return 0

        lax.fori_loop(0, steps, write, 0, unroll=2)

    def widen(a, _):
        taps[pl.ds(pl.multiple_of(2 * OWN * a, 2 * OWN), 2 * OWN), :] = taps_ref[a].astype(f32)
        return 0

    lax.fori_loop(0, BLOCKS, widen, 0, unroll=8)
    blocks = []
    for f in range(OWN):
        parts = [taps[pl.ds(OWN * part + f, BLOCKS, stride=2 * OWN), :] for part in range(2)]
        blocks.append(parts[0] + parts[1])
    for f in range(0, OWN, 2):
        to_lines(blocks[f : f + 2], LINES * f)
    filt[...] = over_rows(forward_ref, 0, OWN).reshape(OWN, LINES, 2 * ROWS)
    extra[...] = jnp.zeros_like(extra)
    lax.fori_loop(0, OWN, main, 0)
    wrap_up()
    leaving(OWN).start()
    for gi in range(OWN + 1):
        leaving(gi).wait()


def extras_kernel(in_ref, spread_ref, mine_ref, other_ref, ext_ref, wide):
    half = lax.axis_index("ch")

    def widen(d, _):
        wide[pl.ds(pl.multiple_of(16 * d, 16), 16), :] = in_ref[d].astype(f32)
        return 0

    lax.fori_loop(0, BLOCKS, widen, 0, unroll=8)
    for k in range(COPIES):
        total = jnp.zeros((32, GROUPS), f32)
        for part in range(2):
            turned = wide[pl.ds(8 * part + k, BLOCKS, stride=16), :].T.astype(bf16)
            for gi in range(OWN):
                total = total + dot(turned[32 * gi : 32 * gi + 32], spread_ref[gi])
        low, high = total[FILTER:, : GROUPS // 2], total[FILTER:, GROUPS // 2 :]
        mine_ref[16 * k : 16 * (k + 1), :] = jnp.where(half == 0, low, high)
        other_ref[16 * k : 16 * (k + 1), :] = jnp.where(half == 0, high, low)
        ext_ref[k] = total[:FILTER]


def finish_kernel(
    in_ref, feat_ref, cot_ref, before_ref, after_ref, weight_ref, ext_ref, mixed_ref, grad_ref, short_ref, skip_ref,
    codes, feat, cot, mixed, grad, wide, code_sem, feat_sem, cot_sem, mixed_sem, grad_sem,
):
    row = lax.broadcasted_iota(jnp.int32, (ROWS, 1), 0)
    share = BLOCKS // 4

    def code_copy(j):
        place = pl.ds(share * j, share)
        return pltpu.make_async_copy(in_ref.at[place, pl.ds(0, RESULT_ROWS), :], codes.at[place], code_sem.at[j])

    def lanes_of(k):
        return pl.ds(pl.multiple_of(GROUPS * k, GROUPS), GROUPS)

    def inputs(k):
        return (
            pltpu.make_async_copy(feat_ref.at[:, :, lanes_of(k)], feat.at[k], feat_sem.at[k]),
            pltpu.make_async_copy(cot_ref.at[:, lanes_of(k)], cot.at[k], cot_sem.at[k]),
        )

    def results(k):
        return (
            pltpu.make_async_copy(mixed.at[k], mixed_ref.at[:, lanes_of(k)], mixed_sem.at[k]),
            pltpu.make_async_copy(grad.at[k], grad_ref.at[:, :, lanes_of(k)], grad_sem.at[k]),
        )

    for j in range(4):
        code_copy(j).start()
    for k in range(COPIES):
        for copy in inputs(k):
            copy.start()
    for j in range(4):
        code_copy(j).wait()

        def widen(d, _):
            place = pl.ds(pl.multiple_of(RESULT_ROWS * d, RESULT_ROWS), RESULT_ROWS)
            wide[place, :] = codes[d].astype(f32)
            return 0

        lax.fori_loop(share * j, share * (j + 1), widen, 0, unroll=8)

    def one(k, _):
        lanes = lanes_of(k)
        for copy in inputs(k):
            copy.wait()
        for i in range(3):
            short_ref[i, :, lanes] = ext_ref[k, TOTAL + 3 * i : TOTAL + 3 * i + 3, :]
        skip_ref[:, lanes] = ext_ref[k, TOTAL + 9 : TOTAL + 10, :]
        signals = []
        for slot in range(2):
            code = wide[pl.ds(8 * slot + k, GROUPS, stride=16), :].T
            signals.append(decode(code, ext_ref[k, SCALE + slot : SCALE + slot + 1, :]))
        conv, grad_mixer = signals
        upstream = cot[k].astype(f32)
        shaped, shaped_after, weights = [], [], []
        for i in range(3):
            taps = [weight_ref[i, j : j + 1, lanes] for j in range(3)]
            weights.append(taps)
            value = feat[k, i].astype(f32)
            before = before_ref[i, :, lanes].astype(f32)
            after = after_ref[i, :, lanes].astype(f32)
            one = jnp.where(row == 0, before[1:2], pltpu.roll(value, 1, 0))
            two = jnp.where(row == 0, before[0:1], jnp.where(row == 1, before[1:2], pltpu.roll(value, 2, 0)))
            shaped.append(taps[0] * value + taps[1] * one + taps[2] * two)
            final, second = value[ROWS - 1 : ROWS], value[ROWS - 2 : ROWS - 1]
            shaped_after.append(
                (
                    taps[0] * after[0:1] + taps[1] * final + taps[2] * second,
                    taps[0] * after[1:2] + taps[1] * after[0:1] + taps[2] * final,
                )
            )
        mixed[k] = (shaped[0] * conv).astype(bf16)
        grads = (upstream * conv, grad_mixer * shaped[2], grad_mixer * shaped[1])
        upstream_after = after_ref[0, :, lanes].astype(f32)
        for i in range(3):
            slope = grads[i]
            following = []
            for t in range(2):
                conv_t = ext_ref[k, AFTER + t : AFTER + t + 1, :]
                mixer_t = ext_ref[k, AFTER + 2 + t : AFTER + 3 + t, :]
                if i == 0:
                    following.append(upstream_after[t : t + 1] * conv_t)
                else:
                    following.append(mixer_t * shaped_after[3 - i][t])
            one = jnp.where(row == ROWS - 1, following[0], pltpu.roll(slope, ROWS - 1, 0))
            two = jnp.where(
                row == ROWS - 1,
                following[1],
                jnp.where(row == ROWS - 2, following[0], pltpu.roll(slope, ROWS - 2, 0)),
            )
            grad[k, i] = weights[i][0] * slope + weights[i][1] * one + weights[i][2] * two
        for copy in results(k):
            copy.start()
        return 0

    lax.fori_loop(0, COPIES, one, 0)
    for k in range(COPIES):
        for copy in results(k):
            copy.wait()


def exchange(values):
    return lax.all_to_all(values, "ctx", split_axis=0, concat_axis=0, tiled=True)


def shift(block, distance):
    route = [(i, i + distance) for i in range(BLOCKS) if 0 <= i + distance < BLOCKS]
    return lax.ppermute(block, "ctx", route)


def pack(features, cotangent, long_filter):
    anywhere = pl.BlockSpec(memory_space=pl.ANY)
    return pl.pallas_call(
        pack_kernel,
        in_specs=[anywhere] * 3,
        out_specs=anywhere,
        out_shape=jax.ShapeDtypeStruct((BLOCKS, SEND_ROWS, ROWS), bf16),
        scratch_shapes=[
            pltpu.VMEM((COPIES, 3, ROWS, GROUPS), bf16),
            pltpu.VMEM((COPIES, ROWS, GROUPS), bf16),
            pltpu.VMEM((ROWS, GROUPS), f32),
            pltpu.VMEM((BLOCKS, SEND_ROWS, ROWS), bf16),
            pltpu.VMEM((4, COPIES * SPACING, ROWS), f32),
            pltpu.VMEM((2, GROUPS, ROWS), f32),
            pltpu.SemaphoreType.DMA((COPIES,)),
            pltpu.SemaphoreType.DMA((COPIES,)),
            pltpu.SemaphoreType.DMA,
            pltpu.SemaphoreType.DMA((4,)),
        ],
        compiler_params=LIMIT,
        name="pack",
    )(features, cotangent, long_filter)


def convolve(gathered, own):
    constants = tables()
    anywhere = pl.BlockSpec(memory_space=pl.ANY)
    whole = lambda array: pl.BlockSpec(array.shape, lambda i: (0,) * array.ndim)
    return pl.pallas_call(
        conv_kernel,
        grid=(1,),
        in_specs=[
            anywhere,
            pl.BlockSpec((BLOCKS, 2 * OWN, ROWS), lambda i: (0, SIGNAL_ROWS // (2 * OWN), 0)),
            whole(own),
        ]
        + [whole(array) for array in constants],
        out_specs=anywhere,
        out_shape=jax.ShapeDtypeStruct((BLOCKS, BACK_ROWS, ROWS), bf16),
        scratch_shapes=[
            pltpu.VMEM((OWN, BLOCKS, 4 * COPIES, ROWS), bf16),
            pltpu.VMEM((OWN + 1, BLOCKS, 2 * COPIES, ROWS), bf16),
            pltpu.SemaphoreType.DMA((OWN,)),
            pltpu.SemaphoreType.DMA((OWN + 1,)),
            pltpu.VMEM((COPIES * BLOCKS, ROWS), f32),
            pltpu.VMEM((COPIES * BLOCKS, ROWS), f32),
            pltpu.VMEM((BLOCKS, 24, ROWS), f32),
            pltpu.VMEM((BLOCKS, 24, ROWS), f32),
            pltpu.VMEM((2 * COPIES * LINES, 2 * ROWS), bf16),
            pltpu.VMEM((2 * COPIES * LINES, 2 * ROWS), bf16),
            pltpu.VMEM((2 * COPIES * LINES, 2 * ROWS), f32),
            pltpu.VMEM((OWN, LINES, 2 * ROWS), f32),
            pltpu.VMEM((OWN, LINES, 2 * ROWS), f32),
            pltpu.VMEM((BLOCKS + 1, COPIES, ROWS), f32),
            pltpu.VMEM((2 * OWN * BLOCKS, ROWS), f32),
            pltpu.VMEM((OWN, COPIES, ROWS), f32),
            pltpu.VMEM((OWN, COPIES * BLOCKS, ROWS), f32),
        ],
        compiler_params=LIMIT,
        name="conv",
    )(gathered, gathered, own, *constants)


def unpack_extras(home):
    spread = np.zeros((OWN, BLOCKS, GROUPS), ml_dtypes.bfloat16)
    for gi in range(OWN):
        spread[gi, np.arange(BLOCKS), OWN * np.arange(BLOCKS) + gi] = 1.0
    return pl.pallas_call(
        extras_kernel,
        grid=(1,),
        in_specs=[
            pl.BlockSpec((BLOCKS, 2 * COPIES, ROWS), lambda i: (0, RESULT_ROWS // (2 * COPIES), 0)),
            pl.BlockSpec((OWN, BLOCKS, GROUPS), lambda i: (0, 0, 0)),
        ],
        out_specs=[
            pl.BlockSpec((ROWS, GROUPS // 2), lambda i: (0, 0)),
            pl.BlockSpec((ROWS, GROUPS // 2), lambda i: (0, 0)),
            pl.BlockSpec((COPIES, FILTER, GROUPS), lambda i: (0, 0, 0)),
        ],
        out_shape=[
            jax.ShapeDtypeStruct((ROWS, GROUPS // 2), f32),
            jax.ShapeDtypeStruct((ROWS, GROUPS // 2), f32),
            jax.ShapeDtypeStruct((COPIES, FILTER, GROUPS), f32),
        ],
        scratch_shapes=[pltpu.VMEM((16 * BLOCKS, ROWS), f32)],
        compiler_params=LIMIT,
        name="extras",
    )(home, spread)


def finish(home, features, cotangent, before, after, short_weight, ext):
    breadth = features.shape[2]
    anywhere = pl.BlockSpec(memory_space=pl.ANY)
    whole = lambda *shape: pl.BlockSpec(shape, lambda i: (0,) * len(shape))
    return pl.pallas_call(
        finish_kernel,
        grid=(1,),
        in_specs=[anywhere] * 3 + [whole(*array.shape) for array in (before, after, short_weight, ext)],
        out_specs=[anywhere, anywhere, whole(3, 3, breadth), whole(1, breadth)],
        out_shape=[
            jax.ShapeDtypeStruct((ROWS, breadth), bf16),
            jax.ShapeDtypeStruct((3, ROWS, breadth), f32),
            jax.ShapeDtypeStruct((3, 3, breadth), f32),
            jax.ShapeDtypeStruct((1, breadth), f32),
        ],
        scratch_shapes=[
            pltpu.VMEM((BLOCKS, RESULT_ROWS, ROWS), bf16),
            pltpu.VMEM((COPIES, 3, ROWS, GROUPS), bf16),
            pltpu.VMEM((COPIES, ROWS, GROUPS), bf16),
            pltpu.VMEM((COPIES, ROWS, GROUPS), bf16),
            pltpu.VMEM((COPIES, 3, ROWS, GROUPS), f32),
            pltpu.VMEM((RESULT_ROWS * BLOCKS, ROWS), f32),
            pltpu.SemaphoreType.DMA((4,)),
        ]
        + [pltpu.SemaphoreType.DMA((COPIES,))] * 4,
        compiler_params=LIMIT,
        name="finish",
    )(home, features, cotangent, before, after, short_weight, ext)


def shards(features, short_weight, skip, long_filter, cotangent):
    rank = lax.axis_index("ctx")
    breadth = features.shape[2]

    gathered = exchange(pack(features, cotangent, long_filter))

    before = shift(features[:, ROWS - 2 :, :], 1)
    after = shift(jnp.concatenate([cotangent[None, :2], features[1:, :2]], axis=0), -1)

    weights = jnp.concatenate([short_weight.reshape(9, breadth), skip[None]], axis=0)
    own = lax.dynamic_index_in_dim(weights.reshape(10, COPIES, BLOCKS, OWN), rank, 2, keepdims=False)
    own = jnp.broadcast_to(jnp.transpose(own, (2, 0, 1))[..., None], (OWN, 10, COPIES, ROWS))

    gathered, own, before, after = lax.optimization_barrier((gathered, own, before, after))
    home = exchange(convolve(gathered, own))

    mine, other, ext = unpack_extras(home)
    arrived = lax.ppermute(other, "ch", [(0, 1), (1, 0)])
    mixed, feature_gradient, grad_short, grad_skip = finish(
        home, features, cotangent, before, after, short_weight, ext
    )
    return (mixed, feature_gradient, grad_short, grad_skip.reshape(breadth), mine + arrived)


def solution(mesh):
    return jax.shard_map(
        shards,
        mesh=mesh,
        in_specs=(
            P(None, "ctx", "ch"),
            P(None, None, "ch"),
            P("ch"),
            P("ctx", None),
            P("ctx", "ch"),
        ),
        out_specs=(
            P("ctx", "ch"),
            P(None, "ctx", "ch"),
            P(None, None, "ch"),
            P("ch"),
            P("ctx", "ch"),
        ),
        check_vma=False,
    )
```

```python
import functools
import math

import jax
import jax.numpy as jnp
import ml_dtypes
import numpy as np
from jax import lax
from jax.experimental import pallas as pl
from jax.experimental.pallas import tpu as pltpu
from jax.sharding import PartitionSpec as P

f32 = jnp.float32
bf16 = jnp.bfloat16

BLOCKS = 64
ROWS = 128
COPIES = 8
GROUPS = 256
OWN = GROUPS // BLOCKS
LINES = 72
PERIOD = 2 * BLOCKS * ROWS
SIGNAL_ROWS = OWN * 4 * COPIES
SEND_ROWS = SIGNAL_ROWS + 2 * OWN
RESULT_ROWS = OWN * 2 * COPIES
BACK_ROWS = RESULT_ROWS + 2 * COPIES
AFTER, SCALE, TOTAL, FILTER = 0, 4, 6, 16
LEVELS = 250.0
BIAS = 125.0
GANG = 8
SPACING = GROUPS + 1
LIMIT = pltpu.CompilerParams(vmem_limit_bytes=32 * 2**20)
ROOMY = pltpu.CompilerParams(vmem_limit_bytes=60 * 2**20)


def high_low(values):
    high = values.astype(ml_dtypes.bfloat16)
    low = (values - high.astype(np.float64)).astype(ml_dtypes.bfloat16)
    return high, low


def tables():
    k1 = np.arange(65)
    a = np.arange(BLOCKS)
    b = np.arange(ROWS)
    turn = 2.0 * np.pi * (k1[:, None] * a[None, :] % ROWS) / ROWS
    first = np.zeros((2 * LINES, BLOCKS))
    first[:65] = np.cos(turn)
    first[LINES : LINES + 65] = -np.sin(turn)
    weight = np.where((k1 == 0) | (k1 == 64), 1.0, 2.0)[:, None] / PERIOD
    last = np.zeros((BLOCKS, 2 * LINES))
    last[:, :65] = (weight * np.cos(turn)).T
    last[:, LINES : LINES + 65] = (-weight * np.sin(turn)).T
    twiddle = np.zeros((2, LINES, ROWS))
    twiddle[0, :65] = np.cos(2.0 * np.pi * k1[:, None] * b[None, :] / PERIOD)
    twiddle[1, :65] = np.sin(2.0 * np.pi * k1[:, None] * b[None, :] / PERIOD)
    angle = 2.0 * np.pi * (b[:, None] * b[None, :] % ROWS) / ROWS
    cosine, sine = np.cos(angle), np.sin(angle)
    forward = np.block([[cosine, -sine], [sine, cosine]])
    first_h, first_l = high_low(first)
    last_h, last_l = high_low(last)
    forward_h, forward_l = high_low(forward)
    return (
        np.concatenate([first_h, first_h, first_l], axis=1),
        np.concatenate([last_h, last_h, last_l], axis=1),
        twiddle.astype(np.float32),
        np.concatenate([forward_h, forward_h, forward_l], axis=0),
    )


def split(values):
    high = values.astype(bf16)
    return high, (values - high.astype(f32)).astype(bf16)


def dot(left, right):
    return jnp.dot(left, right, preferred_element_type=f32)


def encode(values, scale):
    code = jnp.exp2(jnp.abs(values) * (LEVELS / scale) - BIAS)
    return jnp.where(values < 0.0, -code, code).astype(bf16)


def decode(code, scale):
    step = scale * (1.0 / LEVELS)
    value = jnp.log(jnp.abs(code)) * (step * (1.0 / math.log(2.0))) + step * BIAS
    return jnp.where(code < 0.0, -value, value)


def pack_kernel(
    feat_ref, cot_ref, filt_ref, out_ref, feat, cot, filt, packed, turned, taps, feat_sem, cot_sem, filt_sem, out_sem
):
    arriving = []
    for k in range(COPIES):
        lanes = pl.ds(GROUPS * k, GROUPS)
        arriving.append(
            (
                pltpu.make_async_copy(feat_ref.at[:, :, lanes], feat.at[k], feat_sem.at[k]),
                pltpu.make_async_copy(cot_ref.at[:, lanes], cot.at[k], cot_sem.at[k]),
            )
        )
    filter_copy = pltpu.make_async_copy(filt_ref, filt, filt_sem)
    filter_copy.start()
    for copies in arriving:
        for copy in copies:
            copy.start()

    filter_copy.wait()
    value = filt[...].T
    high = value.astype(bf16).astype(f32)
    taps[0] = high
    taps[1] = value - high
    for k in range(COPIES):
        for copy in arriving[k]:
            copy.wait()
        for part in range(4):
            source = cot[k] if part == 3 else feat[k, part]
            turned[part, SPACING * k : SPACING * k + GROUPS, :] = source.astype(f32).T

    def one(d, _):
        for gi in range(OWN):
            n = OWN * d + gi
            tiles = [turned.at[part][pl.ds(n, COPIES, stride=SPACING), :] for part in range(4)]
            packed[d, 32 * gi : 32 * gi + 16, :] = jnp.concatenate(tiles[:2], axis=0).astype(bf16)
            packed[d, 32 * gi + 16 : 32 * gi + 32, :] = jnp.concatenate(tiles[2:], axis=0).astype(bf16)
        pieces = [taps[part, pl.ds(OWN * d, OWN), :] for part in range(2)]
        packed[d, SIGNAL_ROWS:SEND_ROWS, :] = jnp.concatenate(pieces, axis=0).astype(bf16)
        return 0

    leaving = []
    share = BLOCKS // 4
    for j in range(4):
        lax.fori_loop(share * j, share * (j + 1), one, 0, unroll=4)
        place = pl.ds(share * j, share)
        leaving.append(pltpu.make_async_copy(packed.at[place], out_ref.at[place], out_sem.at[j]))
        leaving[-1].start()
    for copy in leaving:
        copy.wait()


def conv_kernel(
    in_ref, taps_ref, weight_ref, first_ref, last_ref, twiddle_ref, forward_ref, out_ref,
    raw_buf, code_buf, in_sem, out_sem,
    left, right, shift_one, shift_two, formed, spec_high, spec_low, lines, filt, cross, extra, taps, totals, own,
):
    chunk = 8
    steps = BLOCKS // chunk
    lane = lax.broadcasted_iota(jnp.int32, (1, 1, ROWS), 2)
    flat = lane[0]
    cosine, sine = twiddle_ref[0], twiddle_ref[1]

    def arriving(gi):
        rows = pl.ds(pl.multiple_of(4 * COPIES * gi, 4 * COPIES), 4 * COPIES)
        return pltpu.make_async_copy(in_ref.at[:, rows, :], raw_buf.at[gi], in_sem.at[gi])

    def leaving(gi):
        rows = pl.ds(pl.multiple_of(2 * COPIES * gi, 2 * COPIES), 2 * COPIES)
        return pltpu.make_async_copy(code_buf.at[gi], out_ref.at[:, rows, :], out_sem.at[gi])

    for gi in range(OWN):
        arriving(gi).start()

    rank = lax.axis_index("ctx")
    column = lax.broadcasted_iota(jnp.int32, (1, GROUPS), 1)
    own_weights = []
    for gi in range(OWN):
        mine = column == OWN * rank + gi
        own_weights.append(
            [jnp.sum(jnp.where(mine, weight_ref[i], 0.0), axis=1, keepdims=True) for i in range(10)]
        )

    def tile_rows(a0):
        return pl.ds(pl.multiple_of(COPIES * a0, 64), COPIES * chunk)

    def shape(weights, signals):
        shaped = []
        for i in range(3):
            rows = slice(8 * i, 8 * i + 8)
            shaped.append(sum(weights[3 * i + j] * signals[j][:, rows] for j in range(3)))
        return shaped

    def pick(ref, k):
        return ref[pl.ds(k, BLOCKS, stride=COPIES), :]

    def to_lines(blocks, base):
        both = jnp.concatenate(blocks, axis=1)
        high, low = split(both)
        mid = dot(first_ref[...], jnp.concatenate([high, low, high], axis=0))
        out = []
        for j in range(2):
            real = mid[:LINES, ROWS * j : ROWS * (j + 1)]
            imag = mid[LINES:, ROWS * j : ROWS * (j + 1)]
            out.append(jnp.concatenate([real * cosine + imag * sine, imag * cosine - real * sine], axis=1))
        keep(jnp.concatenate(out, axis=0), base)

    def keep(values, base):
        high, low = split(values)
        spec_high[base : base + 2 * LINES, :] = high
        spec_low[base : base + 2 * LINES, :] = low

    def over_rows(begin, count):
        rows = slice(LINES * begin, LINES * (begin + count))
        high = spec_high[rows, :]
        return dot(jnp.concatenate([high, spec_low[rows, :], high], axis=1), forward_ref[...])

    def from_lines(values):
        pieces = []
        for j in range(2):
            imag = values[LINES * j : LINES * (j + 1), :ROWS]
            real = values[LINES * j : LINES * (j + 1), ROWS:]
            pieces.append(jnp.concatenate([real * cosine - imag * sine, imag * cosine + real * sine], axis=0))
        high, low = split(jnp.concatenate(pieces, axis=1))
        both = dot(last_ref[...], jnp.concatenate([high, low, high], axis=0))
        return both[:, :ROWS], both[:, ROWS:]

    def spin(values, amount):
        return pltpu.roll(values, amount, values.ndim - 1) if amount else values

    def shape_steps(gi):
        weights = own_weights[gi]
        carry = [jnp.zeros((24, ROWS), f32)] * 2
        mix, grad, ones, twos, forms = (ref.at[gi % 2] for ref in (left, right, shift_one, shift_two, formed))

        def step(a0):
            if a0 == 0:
                arriving(gi).wait()
            raw = raw_buf[gi, a0 : a0 + chunk].astype(f32)
            signal = raw[:, :24]
            one = pltpu.roll(signal, 1, 2)
            two = pltpu.roll(signal, 2, 2)
            one_before = jnp.concatenate([carry[0][None], one[:-1]], axis=0)
            two_before = jnp.concatenate([carry[1][None], two[:-1]], axis=0)
            delayed = (jnp.where(lane < 1, one_before, one), jnp.where(lane < 2, two_before, two))
            ones[a0 : a0 + chunk] = delayed[0]
            twos[a0 : a0 + chunk] = delayed[1]
            shaped = shape(weights, (signal,) + delayed)
            forms[a0 : a0 + chunk] = jnp.concatenate(shaped, axis=1)
            rows = slice(COPIES * a0, COPIES * (a0 + chunk))
            mix[rows, :] = (shaped[1] * shaped[2]).reshape(COPIES * chunk, ROWS)
            grad[rows, :] = (raw[:, 24:] * shaped[0]).reshape(COPIES * chunk, ROWS)
            carry[:] = [one[-1], two[-1]]

        return [functools.partial(step, a0) for a0 in range(0, BLOCKS, chunk)]

    def finish_steps(gi):
        weights = own_weights[gi]
        sums = [jnp.zeros((COPIES, ROWS), f32)] * 10
        last_entry = [jnp.zeros((COPIES, ROWS), f32)]
        mix, grad, ones, twos, forms = (ref.at[gi % 2] for ref in (left, right, shift_one, shift_two, formed))

        def step(a0):
            rows = slice(COPIES * a0, COPIES * (a0 + chunk))
            raw = raw_buf[gi, a0 : a0 + chunk].astype(f32)
            upstream = raw[:, 24:]
            signals = (raw[:, :24], ones[a0 : a0 + chunk], twos[a0 : a0 + chunk])
            shaped = [forms[a0 : a0 + chunk, 8 * i : 8 * i + 8] for i in range(3)]
            mixer = shaped[1] * shaped[2]
            grad_conv = upstream * shaped[0]
            conv = mix[rows, :].reshape(chunk, COPIES, ROWS) + weights[9] * mixer
            grad_mixer = grad[rows, :].reshape(chunk, COPIES, ROWS) + weights[9] * grad_conv
            grads = (upstream * conv, grad_mixer * shaped[2], grad_mixer * shaped[1])
            for i in range(3):
                for j in range(3):
                    sums[3 * i + j] += jnp.sum(grads[i] * signals[j][:, 8 * i : 8 * i + 8], axis=0)
            sums[9] += jnp.sum(grad_conv * mixer, axis=0)

            codes = []
            entry = jnp.zeros((COPIES, ROWS), f32)
            for slot, value in ((0, conv), (1, grad_mixer)):
                largest = jnp.max(jnp.max(jnp.abs(value), axis=0), axis=1, keepdims=True)
                scale = (jnp.maximum(largest, 1e-30) * (1.0 + 1.0 / 128.0)).astype(bf16).astype(f32)
                codes.append(encode(value, scale))
                entry = entry + jnp.where(flat == 32 * gi + SCALE + slot, scale, 0.0)
            code_buf[gi, a0 : a0 + chunk] = jnp.concatenate(codes, axis=1)
            ahead = jnp.where(lane < 2, conv, jnp.where(lane < 4, pltpu.roll(grad_mixer, 2, 2), 0.0))
            entries = [last_entry[0][None]] + [entry[None]] * (chunk - 1)
            update = spin(ahead, 32 * gi) + jnp.concatenate(entries, axis=0)
            extra[a0 : a0 + chunk] = update if gi == 0 else extra[a0 : a0 + chunk] + update
            last_entry[0] = entry
            if a0 + chunk == BLOCKS:
                extra[BLOCKS] = entry if gi == 0 else extra[BLOCKS] + entry
                leaving(gi).start()
                total = jnp.zeros((COPIES, ROWS), f32)
                for i in range(10):
                    value = jnp.sum(sums[i], axis=1, keepdims=True) * (1.0 / math.sqrt(BLOCKS * ROWS))
                    total = total + jnp.where(flat == 32 * gi + TOTAL + i, value, 0.0)
                totals[gi] = total

        return [functools.partial(step, a0) for a0 in range(0, BLOCKS, chunk)]

    def take(steps):
        if steps:
            steps.pop(0)()

    def main(gi, before, after):
        mix, grad = left.at[gi % 2], right.at[gi % 2]
        for base, ref in ((0, mix), (COPIES, grad)):
            for k in range(0, COPIES, GANG):
                for j in range(k, k + GANG, 2):
                    to_lines([pick(ref, j), pick(ref, j + 1)], LINES * (base + j))
                    take(before)
                lines[LINES * (base + k) : LINES * (base + k + GANG), :] = over_rows(base + k, GANG)

        filt_real, filt_imag = filt[gi, :, :ROWS], filt[gi, :, ROWS:]
        cross_real = jnp.zeros((LINES, ROWS), f32)
        cross_imag = jnp.zeros((LINES, ROWS), f32)
        for pair in range(COPIES // 2):
            forth, back = [], []
            for k in (2 * pair, 2 * pair + 1):
                here = slice(LINES * k, LINES * (k + 1))
                there = slice(LINES * (COPIES + k), LINES * (COPIES + k + 1))
                mix_real, mix_imag = lines[here, :ROWS], lines[here, ROWS:]
                grad_real, grad_imag = lines[there, :ROWS], lines[there, ROWS:]
                forth.append(
                    jnp.concatenate(
                        [mix_real * filt_imag + mix_imag * filt_real, mix_real * filt_real - mix_imag * filt_imag], axis=1
                    )
                )
                back.append(
                    jnp.concatenate(
                        [
                            grad_imag * filt_real - grad_real * filt_imag,
                            grad_real * filt_real + grad_imag * filt_imag,
                        ],
                        axis=1,
                    )
                )
                cross_real = cross_real + grad_real * mix_real + grad_imag * mix_imag
                cross_imag = cross_imag + grad_imag * mix_real - grad_real * mix_imag
            keep(jnp.concatenate(forth, axis=0), 2 * LINES * pair)
            keep(jnp.concatenate(back, axis=0), 2 * LINES * (COPIES // 2 + pair))
        cross[gi] = jnp.concatenate([cross_imag, cross_real], axis=1)
        for k in range(0, COPIES, GANG):
            for target, base in ((mix, 0), (grad, COPIES)):
                values = over_rows(base + k, GANG)
                for j in range(0, GANG, 2):
                    pair = from_lines(values[LINES * j : LINES * (j + 2), :])
                    for i in range(2):
                        target[pl.ds(k + j + i, BLOCKS, stride=COPIES), :] = pair[i]
                    take(after)

    def filter_gradient():
        for f in range(0, OWN, 2):
            keep(cross[f : f + 2].reshape(2 * LINES, 2 * ROWS), LINES * f)
        temporal = over_rows(0, OWN)
        scale = 1.0 / math.sqrt(BLOCKS * ROWS * 2 * COPIES)
        for f in range(0, OWN, 2):
            both = from_lines(temporal[LINES * f : LINES * (f + 2)])
            for j in range(2):
                value = both[j] * scale
                for k in range(COPIES):
                    moved = pltpu.roll(value, (32 * (f + j) + FILTER - 16 * k) % ROWS, 1)
                    own.at[f + j][pl.ds(k, BLOCKS, stride=COPIES), :] = moved

    def wrap_up():
        every = totals[0] + totals[1] + totals[2] + totals[3]

        def write(step, _):
            a0 = chunk * step
            value = extra[pl.ds(a0 + 1, chunk)] + every[None]
            for f in range(OWN):
                inside = (lane >= 32 * f + FILTER) & (lane < 32 * f + 32)
                value = jnp.where(inside, own[f, tile_rows(a0), :].reshape(chunk, COPIES, ROWS), value)
            high = value.astype(bf16).astype(f32)
            code_buf[OWN, pl.ds(a0, chunk)] = jnp.concatenate([high, value - high], axis=1).astype(bf16)
            return 0

        lax.fori_loop(0, steps, write, 0, unroll=4)

    def widen(a, _):
        taps[pl.ds(pl.multiple_of(2 * OWN * a, 2 * OWN), 2 * OWN), :] = taps_ref[a].astype(f32)
        return 0

    lax.fori_loop(0, BLOCKS, widen, 0, unroll=8)
    blocks = []
    for f in range(OWN):
        parts = [taps[pl.ds(OWN * part + f, BLOCKS, stride=2 * OWN), :] for part in range(2)]
        blocks.append(parts[0] + parts[1])
    for f in range(0, OWN, 2):
        to_lines(blocks[f : f + 2], LINES * f)
    filt[...] = over_rows(0, OWN).reshape(OWN, LINES, 2 * ROWS)
    for step in shape_steps(0):
        step()
    before = []
    for gi in range(OWN):
        after = shape_steps(gi + 1) if gi + 1 < OWN else []
        main(gi, before, after)
        before = finish_steps(gi)
    filter_gradient()
    for step in before:
        step()
    wrap_up()
    leaving(OWN).start()
    for gi in range(OWN + 1):
        leaving(gi).wait()


def extras_kernel(in_ref, spread_ref, mine_ref, other_ref, ext_ref, wide):
    half = lax.axis_index("ch")

    def widen(d, _):
        wide[pl.ds(pl.multiple_of(16 * d, 16), 16), :] = in_ref[d].astype(f32)
        return 0

    lax.fori_loop(0, BLOCKS, widen, 0, unroll=8)
    turned = [wide[pl.ds(n, BLOCKS, stride=16), :].T.astype(bf16) for n in range(2 * COPIES)]
    total = jnp.zeros((2 * COPIES * 32, GROUPS), f32)
    for gi in range(OWN):
        rows = slice(32 * gi, 32 * gi + 32)
        total = total + dot(jnp.concatenate([piece[rows] for piece in turned], axis=0), spread_ref[gi])
    for k in range(COPIES):
        value = total[32 * k : 32 * k + 32] + total[32 * (COPIES + k) : 32 * (COPIES + k) + 32]
        low, high = value[FILTER:, : GROUPS // 2], value[FILTER:, GROUPS // 2 :]
        mine_ref[16 * k : 16 * (k + 1), :] = jnp.where(half == 0, low, high)
        other_ref[16 * k : 16 * (k + 1), :] = jnp.where(half == 0, high, low)
        ext_ref[k] = value[:FILTER]


def finish_kernel(
    in_ref, feat_ref, cot_ref, before_ref, after_ref, weight_ref, ext_ref, mixed_ref, grad_ref, short_ref, skip_ref,
    codes, feat, cot, mixed, grad, wide, turned, padded, slopes, code_sem, feat_sem, cot_sem, mixed_sem, grad_sem,
):
    share = BLOCKS // 4

    def code_copy(j):
        place = pl.ds(share * j, share)
        return pltpu.make_async_copy(in_ref.at[place, pl.ds(0, RESULT_ROWS), :], codes.at[place], code_sem.at[j])

    def lanes_of(k):
        return pl.ds(pl.multiple_of(GROUPS * k, GROUPS), GROUPS)

    def inputs(k):
        return (
            pltpu.make_async_copy(feat_ref.at[:, :, lanes_of(k)], feat.at[k], feat_sem.at[k]),
            pltpu.make_async_copy(cot_ref.at[:, lanes_of(k)], cot.at[k], cot_sem.at[k]),
        )

    def results(k):
        return (
            pltpu.make_async_copy(mixed.at[k], mixed_ref.at[:, lanes_of(k)], mixed_sem.at[k]),
            pltpu.make_async_copy(grad.at[k], grad_ref.at[:, :, lanes_of(k)], grad_sem.at[k]),
        )

    for j in range(4):
        code_copy(j).start()
    for k in range(COPIES):
        for copy in inputs(k):
            copy.start()
    for j in range(4):
        code_copy(j).wait()

        def widen(d, _):
            place = pl.ds(pl.multiple_of(RESULT_ROWS * d, RESULT_ROWS), RESULT_ROWS)
            wide[place, :] = codes[d].astype(f32)
            return 0

        lax.fori_loop(share * j, share * (j + 1), widen, 0, unroll=8)

    def one(k, _):
        lanes = lanes_of(k)
        for copy in inputs(k):
            copy.wait()
        for i in range(3):
            short_ref[i, :, lanes] = ext_ref[k, TOTAL + 3 * i : TOTAL + 3 * i + 3, :]
        skip_ref[:, lanes] = ext_ref[k, TOTAL + 9 : TOTAL + 10, :]
        scales = [ext_ref[k, SCALE + slot : SCALE + slot + 1, :] for slot in range(2)]
        for slot in range(2):
            turned[slot] = wide[pl.ds(8 * slot + k, GROUPS, stride=16), :].T
        taps = [[weight_ref[i, j : j + 1, lanes] for j in range(3)] for i in range(3)]
        for i in range(3):
            padded[i, 6:8, :] = before_ref[i, :, lanes].astype(f32)
            padded[i, 8 : 8 + ROWS, :] = feat[k, i].astype(f32)
            padded[i, 8 + ROWS : 10 + ROWS, :] = after_ref[i, :, lanes].astype(f32)

        def shape(i, begin, size):
            return sum(taps[i][j] * padded[i, 8 + begin - j : 8 + begin - j + size, :] for j in range(3))

        size = 16
        for begin in range(0, ROWS, size):
            rows = slice(begin, begin + size)
            conv, grad_mixer = (decode(turned[slot, rows, :], scales[slot]) for slot in range(2))
            upstream = cot[k, rows, :].astype(f32)
            mixed[k, rows, :] = (shape(0, begin, size) * conv).astype(bf16)
            slopes[0, rows, :] = upstream * conv
            slopes[1, rows, :] = grad_mixer * shape(2, begin, size)
            slopes[2, rows, :] = grad_mixer * shape(1, begin, size)
        following = slice(ROWS, ROWS + 2)
        grad_mixer = ext_ref[k, AFTER + 2 : AFTER + 4, :]
        slopes[0, following, :] = padded[0, 8 + ROWS : 10 + ROWS, :] * ext_ref[k, AFTER : AFTER + 2, :]
        slopes[1, following, :] = grad_mixer * shape(2, ROWS, 2)
        slopes[2, following, :] = grad_mixer * shape(1, ROWS, 2)
        for i in range(3):
            for begin in range(0, ROWS, size):
                grad[k, i, begin : begin + size, :] = sum(
                    taps[i][j] * slopes[i, begin + j : begin + j + size, :] for j in range(3)
                )
        for copy in results(k):
            copy.start()
        return 0

    lax.fori_loop(0, COPIES, one, 0)
    for k in range(COPIES):
        for copy in results(k):
            copy.wait()


def exchange(values):
    return lax.all_to_all(values, "ctx", split_axis=0, concat_axis=0, tiled=True)


def shift(block, distance):
    route = [(i, i + distance) for i in range(BLOCKS) if 0 <= i + distance < BLOCKS]
    return lax.ppermute(block, "ctx", route)


def pack(features, cotangent, long_filter):
    anywhere = pl.BlockSpec(memory_space=pl.ANY)
    return pl.pallas_call(
        pack_kernel,
        in_specs=[anywhere] * 3,
        out_specs=anywhere,
        out_shape=jax.ShapeDtypeStruct((BLOCKS, SEND_ROWS, ROWS), bf16),
        scratch_shapes=[
            pltpu.VMEM((COPIES, 3, ROWS, GROUPS), bf16),
            pltpu.VMEM((COPIES, ROWS, GROUPS), bf16),
            pltpu.VMEM((ROWS, GROUPS), f32),
            pltpu.VMEM((BLOCKS, SEND_ROWS, ROWS), bf16),
            pltpu.VMEM((4, COPIES * SPACING, ROWS), f32),
            pltpu.VMEM((2, GROUPS, ROWS), f32),
            pltpu.SemaphoreType.DMA((COPIES,)),
            pltpu.SemaphoreType.DMA((COPIES,)),
            pltpu.SemaphoreType.DMA,
            pltpu.SemaphoreType.DMA((4,)),
        ],
        compiler_params=ROOMY,
        name="pack",
    )(features, cotangent, long_filter)


def convolve(gathered, own):
    constants = tables()
    anywhere = pl.BlockSpec(memory_space=pl.ANY)
    whole = lambda array: pl.BlockSpec(array.shape, lambda i: (0,) * array.ndim)
    return pl.pallas_call(
        conv_kernel,
        grid=(1,),
        in_specs=[
            anywhere,
            pl.BlockSpec((BLOCKS, 2 * OWN, ROWS), lambda i: (0, SIGNAL_ROWS // (2 * OWN), 0)),
            whole(own),
        ]
        + [whole(array) for array in constants],
        out_specs=anywhere,
        out_shape=jax.ShapeDtypeStruct((BLOCKS, BACK_ROWS, ROWS), bf16),
        scratch_shapes=[
            pltpu.VMEM((OWN, BLOCKS, 4 * COPIES, ROWS), bf16),
            pltpu.VMEM((OWN + 1, BLOCKS, 2 * COPIES, ROWS), bf16),
            pltpu.SemaphoreType.DMA((OWN,)),
            pltpu.SemaphoreType.DMA((OWN + 1,)),
            pltpu.VMEM((2, COPIES * BLOCKS, ROWS), f32),
            pltpu.VMEM((2, COPIES * BLOCKS, ROWS), f32),
            pltpu.VMEM((2, BLOCKS, 24, ROWS), f32),
            pltpu.VMEM((2, BLOCKS, 24, ROWS), f32),
            pltpu.VMEM((2, BLOCKS, 24, ROWS), f32),
            pltpu.VMEM((2 * COPIES * LINES, 2 * ROWS), bf16),
            pltpu.VMEM((2 * COPIES * LINES, 2 * ROWS), bf16),
            pltpu.VMEM((2 * COPIES * LINES, 2 * ROWS), f32),
            pltpu.VMEM((OWN, LINES, 2 * ROWS), f32),
            pltpu.VMEM((OWN, LINES, 2 * ROWS), f32),
            pltpu.VMEM((BLOCKS + 1, COPIES, ROWS), f32),
            pltpu.VMEM((2 * OWN * BLOCKS, ROWS), f32),
            pltpu.VMEM((OWN, COPIES, ROWS), f32),
            pltpu.VMEM((OWN, COPIES * BLOCKS, ROWS), f32),
        ],
        compiler_params=LIMIT,
        name="conv",
    )(gathered, gathered, own, *constants)


def unpack_extras(home):
    spread = np.zeros((OWN, BLOCKS, GROUPS), ml_dtypes.bfloat16)
    for gi in range(OWN):
        spread[gi, np.arange(BLOCKS), OWN * np.arange(BLOCKS) + gi] = 1.0
    return pl.pallas_call(
        extras_kernel,
        grid=(1,),
        in_specs=[
            pl.BlockSpec((BLOCKS, 2 * COPIES, ROWS), lambda i: (0, RESULT_ROWS // (2 * COPIES), 0)),
            pl.BlockSpec((OWN, BLOCKS, GROUPS), lambda i: (0, 0, 0)),
        ],
        out_specs=[
            pl.BlockSpec((ROWS, GROUPS // 2), lambda i: (0, 0)),
            pl.BlockSpec((ROWS, GROUPS // 2), lambda i: (0, 0)),
            pl.BlockSpec((COPIES, FILTER, GROUPS), lambda i: (0, 0, 0)),
        ],
        out_shape=[
            jax.ShapeDtypeStruct((ROWS, GROUPS // 2), f32),
            jax.ShapeDtypeStruct((ROWS, GROUPS // 2), f32),
            jax.ShapeDtypeStruct((COPIES, FILTER, GROUPS), f32),
        ],
        scratch_shapes=[pltpu.VMEM((16 * BLOCKS, ROWS), f32)],
        compiler_params=LIMIT,
        name="extras",
    )(home, spread)


def finish(home, features, cotangent, before, after, short_weight, ext):
    breadth = features.shape[2]
    anywhere = pl.BlockSpec(memory_space=pl.ANY)
    whole = lambda *shape: pl.BlockSpec(shape, lambda i: (0,) * len(shape))
    return pl.pallas_call(
        finish_kernel,
        grid=(1,),
        in_specs=[anywhere] * 3 + [whole(*array.shape) for array in (before, after, short_weight, ext)],
        out_specs=[anywhere, anywhere, whole(3, 3, breadth), whole(1, breadth)],
        out_shape=[
            jax.ShapeDtypeStruct((ROWS, breadth), bf16),
            jax.ShapeDtypeStruct((3, ROWS, breadth), f32),
            jax.ShapeDtypeStruct((3, 3, breadth), f32),
            jax.ShapeDtypeStruct((1, breadth), f32),
        ],
        scratch_shapes=[
            pltpu.VMEM((BLOCKS, RESULT_ROWS, ROWS), bf16),
            pltpu.VMEM((COPIES, 3, ROWS, GROUPS), bf16),
            pltpu.VMEM((COPIES, ROWS, GROUPS), bf16),
            pltpu.VMEM((COPIES, ROWS, GROUPS), bf16),
            pltpu.VMEM((COPIES, 3, ROWS, GROUPS), f32),
            pltpu.VMEM((RESULT_ROWS * BLOCKS, ROWS), f32),
            pltpu.VMEM((2, ROWS, GROUPS), f32),
            pltpu.VMEM((3, ROWS + 16, GROUPS), f32),
            pltpu.VMEM((3, ROWS + 8, GROUPS), f32),
            pltpu.SemaphoreType.DMA((4,)),
        ]
        + [pltpu.SemaphoreType.DMA((COPIES,))] * 4,
        compiler_params=LIMIT,
        name="finish",
    )(home, features, cotangent, before, after, short_weight, ext)


def shards(features, short_weight, skip, long_filter, cotangent):
    breadth = features.shape[2]

    gathered = exchange(pack(features, cotangent, long_filter))

    before = shift(features[:, ROWS - 2 :, :], 1)
    after = shift(jnp.concatenate([cotangent[None, :2], features[1:, :2]], axis=0), -1)

    weights = jnp.concatenate([short_weight.reshape(9, breadth), skip[None]], axis=0)
    weights = weights.reshape(10, COPIES, GROUPS)

    gathered, weights, before, after = lax.optimization_barrier((gathered, weights, before, after))
    home = exchange(convolve(gathered, weights))

    mine, other, ext = unpack_extras(home)
    arrived = lax.ppermute(other, "ch", [(0, 1), (1, 0)])
    mixed, feature_gradient, grad_short, grad_skip = finish(
        home, features, cotangent, before, after, short_weight, ext
    )
    return (mixed, feature_gradient, grad_short, grad_skip.reshape(breadth), mine + arrived)


def solution(mesh):
    return jax.shard_map(
        shards,
        mesh=mesh,
        in_specs=(
            P(None, "ctx", "ch"),
            P(None, None, "ch"),
            P("ch"),
            P("ctx", None),
            P("ctx", "ch"),
        ),
        out_specs=(
            P("ctx", "ch"),
            P(None, "ctx", "ch"),
            P(None, None, "ch"),
            P("ch"),
            P("ctx", "ch"),
        ),
        check_vma=False,
    )
```

```python
import functools
import math

import jax
import jax.numpy as jnp
import ml_dtypes
import numpy as np
from jax import lax
from jax.experimental import pallas as pl
from jax.experimental.pallas import tpu as pltpu
from jax.sharding import PartitionSpec as P

f32 = jnp.float32
bf16 = jnp.bfloat16

BLOCKS = 64
ROWS = 128
COPIES = 8
GROUPS = 256
OWN = GROUPS // BLOCKS
LINES = 72
PERIOD = 2 * BLOCKS * ROWS
SIGNAL_ROWS = OWN * 4 * COPIES
SEND_ROWS = SIGNAL_ROWS + 2 * OWN
RESULT_ROWS = OWN * 2 * COPIES
BACK_ROWS = RESULT_ROWS + 2 * COPIES
AFTER, TOTAL, SPLIT = 0, 6, 16
BEFORE, SCALE, FILTER_SCALE = 16, 22, 24
LEVELS = 250.0
BIAS = 125.0
GANG = 8
SPACING = GROUPS + 1
LIMIT = pltpu.CompilerParams(vmem_limit_bytes=32 * 2**20)
ROOMY = pltpu.CompilerParams(vmem_limit_bytes=60 * 2**20)


def high_low(values):
    high = values.astype(ml_dtypes.bfloat16)
    low = (values - high.astype(np.float64)).astype(ml_dtypes.bfloat16)
    return high, low


def tables():
    k1 = np.arange(65)
    a = np.arange(BLOCKS)
    b = np.arange(ROWS)
    turn = 2.0 * np.pi * (k1[:, None] * a[None, :] % ROWS) / ROWS
    first = np.zeros((2 * LINES, BLOCKS))
    first[:65] = np.cos(turn)
    first[LINES : LINES + 65] = -np.sin(turn)
    weight = np.where((k1 == 0) | (k1 == 64), 1.0, 2.0)[:, None] / PERIOD
    last = np.zeros((BLOCKS, 2 * LINES))
    last[:, :65] = (weight * np.cos(turn)).T
    last[:, LINES : LINES + 65] = (-weight * np.sin(turn)).T
    twiddle = np.zeros((2, LINES, ROWS))
    twiddle[0, :65] = np.cos(2.0 * np.pi * k1[:, None] * b[None, :] / PERIOD)
    twiddle[1, :65] = np.sin(2.0 * np.pi * k1[:, None] * b[None, :] / PERIOD)
    angle = 2.0 * np.pi * (b[:, None] * b[None, :] % ROWS) / ROWS
    cosine, sine = np.cos(angle), np.sin(angle)
    forward = np.block([[cosine, -sine], [sine, cosine]])
    first_h, first_l = high_low(first)
    last_h, last_l = high_low(last)
    forward_h, forward_l = high_low(forward)
    return (
        np.concatenate([first_h, first_h, first_l], axis=1),
        np.concatenate([last_h, last_h, last_l], axis=1),
        twiddle.astype(np.float32),
        np.concatenate([forward_h, forward_h, forward_l], axis=0),
    )


def split(values):
    high = values.astype(bf16)
    return high, (values - high.astype(f32)).astype(bf16)


def dot(left, right):
    return jnp.dot(left, right, preferred_element_type=f32)


def encode(values, scale):
    code = jnp.exp2(jnp.abs(values) * (LEVELS / scale) - BIAS)
    return jnp.where(values < 0.0, -code, code)


def scale_of(largest):
    return (jnp.maximum(largest, 1e-30) * (1.0 + 1.0 / 128.0)).astype(bf16).astype(f32)


def decode(code, scale):
    step = scale * (1.0 / LEVELS)
    value = jnp.log(jnp.abs(code)) * (step * (1.0 / math.log(2.0))) + step * BIAS
    return jnp.where(code < 0.0, -value, value)


def pack_kernel(
    feat_ref, cot_ref, filt_ref, out_ref, feat, cot, filt, packed, turned, taps, feat_sem, cot_sem, filt_sem, out_sem
):
    arriving = []
    for k in range(COPIES):
        lanes = pl.ds(GROUPS * k, GROUPS)
        arriving.append(
            (
                pltpu.make_async_copy(feat_ref.at[:, :, lanes], feat.at[k], feat_sem.at[k]),
                pltpu.make_async_copy(cot_ref.at[:, lanes], cot.at[k], cot_sem.at[k]),
            )
        )
    filter_copy = pltpu.make_async_copy(filt_ref, filt, filt_sem)
    filter_copy.start()
    for copies in arriving:
        for copy in copies:
            copy.start()

    filter_copy.wait()
    value = filt[...].T
    high = value.astype(bf16).astype(f32)
    taps[0] = high
    taps[1] = value - high
    for k in range(COPIES):
        for copy in arriving[k]:
            copy.wait()
        for part in range(4):
            source = cot[k] if part == 3 else feat[k, part]
            turned[part, SPACING * k : SPACING * k + GROUPS, :] = source.astype(f32).T

    def one(d, _):
        for gi in range(OWN):
            n = OWN * d + gi
            tiles = [turned.at[part][pl.ds(n, COPIES, stride=SPACING), :] for part in range(4)]
            packed[d, 32 * gi : 32 * gi + 16, :] = jnp.concatenate(tiles[:2], axis=0).astype(bf16)
            packed[d, 32 * gi + 16 : 32 * gi + 32, :] = jnp.concatenate(tiles[2:], axis=0).astype(bf16)
        pieces = [taps[part, pl.ds(OWN * d, OWN), :] for part in range(2)]
        packed[d, SIGNAL_ROWS:SEND_ROWS, :] = jnp.concatenate(pieces, axis=0).astype(bf16)
        return 0

    leaving = []
    share = BLOCKS // 4
    for j in range(4):
        lax.fori_loop(share * j, share * (j + 1), one, 0, unroll=4)
        place = pl.ds(share * j, share)
        leaving.append(pltpu.make_async_copy(packed.at[place], out_ref.at[place], out_sem.at[j]))
        leaving[-1].start()
    for copy in leaving:
        copy.wait()


def conv_kernel(
    in_ref, taps_ref, weight_ref, first_ref, last_ref, twiddle_ref, forward_ref, out_ref,
    raw_buf, code_buf, in_sem, out_sem,
    left, right, shift_one, shift_two, formed, spec_high, spec_low, lines, filt, cross, extra, exact, taps, totals, own, own_scale,
):
    chunk = 8
    steps = BLOCKS // chunk
    lane = lax.broadcasted_iota(jnp.int32, (1, 1, ROWS), 2)
    flat = lane[0]
    cosine, sine = twiddle_ref[0], twiddle_ref[1]

    def arriving(gi):
        rows = pl.ds(pl.multiple_of(4 * COPIES * gi, 4 * COPIES), 4 * COPIES)
        return pltpu.make_async_copy(in_ref.at[:, rows, :], raw_buf.at[gi], in_sem.at[gi])

    def leaving(gi):
        rows = pl.ds(pl.multiple_of(2 * COPIES * gi, 2 * COPIES), 2 * COPIES)
        return pltpu.make_async_copy(code_buf.at[gi], out_ref.at[:, rows, :], out_sem.at[gi])

    for gi in range(OWN):
        arriving(gi).start()

    rank = lax.axis_index("ctx")
    column = lax.broadcasted_iota(jnp.int32, (1, GROUPS), 1)
    own_weights = []
    for gi in range(OWN):
        mine = column == OWN * rank + gi
        own_weights.append(
            [jnp.sum(jnp.where(mine, weight_ref[i], 0.0), axis=1, keepdims=True) for i in range(10)]
        )

    def tile_rows(a0):
        return pl.ds(pl.multiple_of(COPIES * a0, 64), COPIES * chunk)

    def shape(weights, signals):
        shaped = []
        for i in range(3):
            rows = slice(8 * i, 8 * i + 8)
            shaped.append(sum(weights[3 * i + j] * signals[j][:, rows] for j in range(3)))
        return shaped

    def pick(ref, k):
        return ref[pl.ds(k, BLOCKS, stride=COPIES), :]

    def to_lines(blocks, base):
        both = jnp.concatenate(blocks, axis=1)
        high, low = split(both)
        mid = dot(first_ref[...], jnp.concatenate([high, low, high], axis=0))
        out = []
        for j in range(2):
            real = mid[:LINES, ROWS * j : ROWS * (j + 1)]
            imag = mid[LINES:, ROWS * j : ROWS * (j + 1)]
            out.append(jnp.concatenate([real * cosine + imag * sine, imag * cosine - real * sine], axis=1))
        keep(jnp.concatenate(out, axis=0), base)

    def keep(values, base):
        high, low = split(values)
        spec_high[base : base + 2 * LINES, :] = high
        spec_low[base : base + 2 * LINES, :] = low

    def over_rows(begin, count):
        rows = slice(LINES * begin, LINES * (begin + count))
        high = spec_high[rows, :]
        return dot(jnp.concatenate([high, spec_low[rows, :], high], axis=1), forward_ref[...])

    def from_lines(values):
        pieces = []
        for j in range(2):
            imag = values[LINES * j : LINES * (j + 1), :ROWS]
            real = values[LINES * j : LINES * (j + 1), ROWS:]
            pieces.append(jnp.concatenate([real * cosine - imag * sine, imag * cosine + real * sine], axis=0))
        high, low = split(jnp.concatenate(pieces, axis=1))
        both = dot(last_ref[...], jnp.concatenate([high, low, high], axis=0))
        return both[:, :ROWS], both[:, ROWS:]

    def spin(values, amount):
        return pltpu.roll(values, amount, values.ndim - 1) if amount else values

    def shape_steps(gi):
        weights = own_weights[gi]
        carry = [jnp.zeros((24, ROWS), f32)] * 2
        mix, grad, ones, twos, forms = (ref.at[gi % 2] for ref in (left, right, shift_one, shift_two, formed))

        def step(a0):
            if a0 == 0:
                arriving(gi).wait()
            raw = raw_buf[gi, a0 : a0 + chunk].astype(f32)
            signal = raw[:, :24]
            one = pltpu.roll(signal, 1, 2)
            two = pltpu.roll(signal, 2, 2)
            one_before = jnp.concatenate([carry[0][None], one[:-1]], axis=0)
            two_before = jnp.concatenate([carry[1][None], two[:-1]], axis=0)
            delayed = (jnp.where(lane < 1, one_before, one), jnp.where(lane < 2, two_before, two))
            ones[a0 : a0 + chunk] = delayed[0]
            twos[a0 : a0 + chunk] = delayed[1]
            shaped = shape(weights, (signal,) + delayed)
            forms[a0 : a0 + chunk] = jnp.concatenate(shaped, axis=1)
            rows = slice(COPIES * a0, COPIES * (a0 + chunk))
            mix[rows, :] = (shaped[1] * shaped[2]).reshape(COPIES * chunk, ROWS)
            grad[rows, :] = (raw[:, 24:] * shaped[0]).reshape(COPIES * chunk, ROWS)
            carry[:] = [one[-1], two[-1]]

        return [functools.partial(step, a0) for a0 in range(0, BLOCKS, chunk)]

    def finish_steps(gi):
        weights = own_weights[gi]
        sums = [jnp.zeros((COPIES, ROWS), f32)] * 10
        mix, grad, ones, twos, forms = (ref.at[gi % 2] for ref in (left, right, shift_one, shift_two, formed))

        def step(a0):
            rows = slice(COPIES * a0, COPIES * (a0 + chunk))
            raw = raw_buf[gi, a0 : a0 + chunk].astype(f32)
            upstream = raw[:, 24:]
            signals = (raw[:, :24], ones[a0 : a0 + chunk], twos[a0 : a0 + chunk])
            shaped = [forms[a0 : a0 + chunk, 8 * i : 8 * i + 8] for i in range(3)]
            mixer = shaped[1] * shaped[2]
            grad_conv = upstream * shaped[0]
            conv = mix[rows, :].reshape(chunk, COPIES, ROWS) + weights[9] * mixer
            grad_mixer = grad[rows, :].reshape(chunk, COPIES, ROWS) + weights[9] * grad_conv
            grads = (upstream * conv, grad_mixer * shaped[2], grad_mixer * shaped[1])
            for i in range(3):
                for j in range(3):
                    sums[3 * i + j] += jnp.sum(grads[i] * signals[j][:, 8 * i : 8 * i + 8], axis=0)
            sums[9] += jnp.sum(grad_conv * mixer, axis=0)

            codes = []
            entry = jnp.zeros((COPIES, ROWS), f32)
            for slot, value in ((0, conv), (1, grad_mixer)):
                scale = scale_of(jnp.max(jnp.max(jnp.abs(value), axis=0), axis=1, keepdims=True))
                codes.append(encode(value, scale).astype(bf16))
                entry = entry + jnp.where(flat == 32 * gi + SCALE + slot, scale, 0.0)
            code_buf[gi, a0 : a0 + chunk] = jnp.concatenate(codes, axis=1)
            ahead = jnp.zeros((chunk, COPIES, ROWS), f32)
            behind = jnp.broadcast_to(entry, (chunk, COPIES, ROWS))
            for i in range(3):
                place = 32 * gi + AFTER + 2 * i
                ahead = jnp.where((lane >= place) & (lane < place + 2), spin(grads[i], place), ahead)
                place = 32 * gi + BEFORE + 2 * i
                moved = spin(signals[2][:, 8 * i : 8 * i + 8], place)
                behind = jnp.where((lane >= place) & (lane < place + 2), moved, behind)
            here = slice(a0, a0 + chunk)
            extra[here] = ahead if gi == 0 else extra[here] + ahead
            exact[here] = behind if gi == 0 else exact[here] + behind
            if a0 + chunk == BLOCKS:
                leaving(gi).start()
                total = jnp.zeros((COPIES, ROWS), f32)
                for i in range(10):
                    value = jnp.sum(sums[i], axis=1, keepdims=True) * (1.0 / math.sqrt(BLOCKS * ROWS))
                    total = total + jnp.where(flat == 32 * gi + TOTAL + i, value, 0.0)
                totals[gi] = total

        return [functools.partial(step, a0) for a0 in range(0, BLOCKS, chunk)]

    def take(steps):
        if steps:
            steps.pop(0)()

    def main(gi, before, after):
        mix, grad = left.at[gi % 2], right.at[gi % 2]
        for base, ref in ((0, mix), (COPIES, grad)):
            for k in range(0, COPIES, GANG):
                for j in range(k, k + GANG, 2):
                    to_lines([pick(ref, j), pick(ref, j + 1)], LINES * (base + j))
                    take(before)
                lines[LINES * (base + k) : LINES * (base + k + GANG), :] = over_rows(base + k, GANG)

        filt_real, filt_imag = filt[gi, :, :ROWS], filt[gi, :, ROWS:]
        cross_real = jnp.zeros((LINES, ROWS), f32)
        cross_imag = jnp.zeros((LINES, ROWS), f32)
        for pair in range(COPIES // 2):
            forth, back = [], []
            for k in (2 * pair, 2 * pair + 1):
                here = slice(LINES * k, LINES * (k + 1))
                there = slice(LINES * (COPIES + k), LINES * (COPIES + k + 1))
                mix_real, mix_imag = lines[here, :ROWS], lines[here, ROWS:]
                grad_real, grad_imag = lines[there, :ROWS], lines[there, ROWS:]
                forth.append(
                    jnp.concatenate(
                        [mix_real * filt_imag + mix_imag * filt_real, mix_real * filt_real - mix_imag * filt_imag], axis=1
                    )
                )
                back.append(
                    jnp.concatenate(
                        [
                            grad_imag * filt_real - grad_real * filt_imag,
                            grad_real * filt_real + grad_imag * filt_imag,
                        ],
                        axis=1,
                    )
                )
                cross_real = cross_real + grad_real * mix_real + grad_imag * mix_imag
                cross_imag = cross_imag + grad_imag * mix_real - grad_real * mix_imag
            keep(jnp.concatenate(forth, axis=0), 2 * LINES * pair)
            keep(jnp.concatenate(back, axis=0), 2 * LINES * (COPIES // 2 + pair))
        cross[gi] = jnp.concatenate([cross_imag, cross_real], axis=1)
        for k in range(0, COPIES, GANG):
            for target, base in ((mix, 0), (grad, COPIES)):
                values = over_rows(base + k, GANG)
                for j in range(0, GANG, 2):
                    pair = from_lines(values[LINES * j : LINES * (j + 2), :])
                    for i in range(2):
                        target[pl.ds(k + j + i, BLOCKS, stride=COPIES), :] = pair[i]
                    take(after)

    def filter_gradient():
        for f in range(0, OWN, 2):
            keep(cross[f : f + 2].reshape(2 * LINES, 2 * ROWS), LINES * f)
        temporal = over_rows(0, OWN)
        scale = 1.0 / math.sqrt(BLOCKS * ROWS * 2 * COPIES)
        values = []
        for f in range(0, OWN, 2):
            values.extend(from_lines(temporal[LINES * f : LINES * (f + 2)]))
        codes = []
        scales = jnp.zeros((BLOCKS, ROWS), f32)
        for f in range(OWN):
            value = values[f] * scale
            size = scale_of(jnp.max(jnp.abs(value), axis=1, keepdims=True))
            codes.append(encode(value, size))
            scales = jnp.where(flat == 32 * f + FILTER_SCALE, size, scales)
        for k in range(COPIES):
            moved = jnp.zeros((BLOCKS, ROWS), f32)
            for f in range(OWN):
                inside = (flat >= 32 * f + SPLIT) & (flat < 32 * f + 32)
                moved = jnp.where(inside, spin(codes[f], (32 * f + SPLIT - 16 * k) % ROWS), moved)
            own[pl.ds(k, BLOCKS, stride=COPIES), :] = moved
            own_scale[pl.ds(k, BLOCKS, stride=COPIES), :] = scales

    def wrap_up():
        every = totals[0] + totals[1] + totals[2] + totals[3]

        def write(step, _):
            a0 = chunk * step
            value = extra[pl.ds(a0 + 1, chunk)] + every[None]
            high = value.astype(bf16).astype(f32)
            code = own[tile_rows(a0), :].reshape(chunk, COPIES, ROWS)
            single = exact[pl.ds(a0, chunk)] + own_scale[tile_rows(a0), :].reshape(chunk, COPIES, ROWS)
            both = [jnp.where(lane % 32 < SPLIT, high, code), jnp.where(lane % 32 < SPLIT, value - high, single)]
            code_buf[OWN, pl.ds(a0, chunk)] = jnp.concatenate(both, axis=1).astype(bf16)
            return 0

        lax.fori_loop(0, steps, write, 0, unroll=8)

    def widen(a, _):
        taps[pl.ds(pl.multiple_of(2 * OWN * a, 2 * OWN), 2 * OWN), :] = taps_ref[a].astype(f32)
        return 0

    lax.fori_loop(0, BLOCKS, widen, 0, unroll=8)
    blocks = []
    for f in range(OWN):
        parts = [taps[pl.ds(OWN * part + f, BLOCKS, stride=2 * OWN), :] for part in range(2)]
        blocks.append(parts[0] + parts[1])
    for f in range(0, OWN, 2):
        to_lines(blocks[f : f + 2], LINES * f)
    filt[...] = over_rows(0, OWN).reshape(OWN, LINES, 2 * ROWS)
    extra[BLOCKS] = jnp.zeros((COPIES, ROWS), f32)
    for step in shape_steps(0):
        step()
    before = []
    for gi in range(OWN):
        after = shape_steps(gi + 1) if gi + 1 < OWN else []
        main(gi, before, after)
        before = finish_steps(gi)
    filter_gradient()
    for step in before:
        step()
    wrap_up()
    leaving(OWN).start()
    for gi in range(OWN + 1):
        leaving(gi).wait()


def extras_kernel(in_ref, spread_ref, mine_ref, other_ref, ext_ref, wide):
    half = lax.axis_index("ch")

    def widen(d, _):
        wide[pl.ds(pl.multiple_of(16 * d, 16), 16), :] = in_ref[d].astype(f32)
        return 0

    lax.fori_loop(0, BLOCKS, widen, 0, unroll=8)
    turned = [wide[pl.ds(n, BLOCKS, stride=16), :].T.astype(bf16) for n in range(2 * COPIES)]
    total = jnp.zeros((2 * COPIES * 32, GROUPS), f32)
    for gi in range(OWN):
        rows = slice(32 * gi, 32 * gi + 32)
        total = total + dot(jnp.concatenate([piece[rows] for piece in turned], axis=0), spread_ref[gi])
    for k in range(COPIES):
        first = total[32 * k : 32 * k + 32]
        second = total[32 * (COPIES + k) : 32 * (COPIES + k) + 32]
        value = decode(first[SPLIT:], second[FILTER_SCALE : FILTER_SCALE + 1])
        low, high = value[:, : GROUPS // 2], value[:, GROUPS // 2 :]
        mine_ref[16 * k : 16 * (k + 1), :] = jnp.where(half == 0, low, high)
        other_ref[16 * k : 16 * (k + 1), :] = jnp.where(half == 0, high, low)
        ext_ref[k, :SPLIT, :] = first[:SPLIT] + second[:SPLIT]
        ext_ref[k, SPLIT:, :] = second[SPLIT:]


def prepare_kernel(feat_ref, weight_ref, out_ref):
    row = lax.broadcasted_iota(jnp.int32, (ROWS, 1), 0)
    for i in range(3):
        value = feat_ref[i].astype(f32)
        one = jnp.where(row < 1, 0.0, pltpu.roll(value, 1, 0))
        two = jnp.where(row < 2, 0.0, pltpu.roll(value, 2, 0))
        out_ref[i] = weight_ref[i, 0:1, :] * value + weight_ref[i, 1:2, :] * one + weight_ref[i, 2:3, :] * two


def finish_kernel(
    in_ref, shaped_ref, cot_ref, weight_ref, ext_ref, mixed_ref, grad_ref, short_ref, skip_ref,
    codes, shaped, cot, mixed, grad, wide, turned, code_sem, shaped_sem, cot_sem, mixed_sem, grad_sem,
):
    share = BLOCKS // 4

    def code_copy(j):
        place = pl.ds(share * j, share)
        return pltpu.make_async_copy(in_ref.at[place, pl.ds(0, RESULT_ROWS), :], codes.at[place], code_sem.at[j])

    def lanes_of(k):
        return pl.ds(pl.multiple_of(GROUPS * k, GROUPS), GROUPS)

    def inputs(k):
        return (
            pltpu.make_async_copy(shaped_ref.at[:, :, lanes_of(k)], shaped.at[k], shaped_sem.at[k]),
            pltpu.make_async_copy(cot_ref.at[:, lanes_of(k)], cot.at[k], cot_sem.at[k]),
        )

    def results(k):
        return (
            pltpu.make_async_copy(mixed.at[k], mixed_ref.at[:, lanes_of(k)], mixed_sem.at[k]),
            pltpu.make_async_copy(grad.at[k], grad_ref.at[:, :, lanes_of(k)], grad_sem.at[k]),
        )

    for j in range(4):
        code_copy(j).start()
    for k in range(COPIES):
        for copy in inputs(k):
            copy.start()
    for j in range(4):
        code_copy(j).wait()

        def widen(d, _):
            place = pl.ds(pl.multiple_of(RESULT_ROWS * d, RESULT_ROWS), RESULT_ROWS)
            wide[place, :] = codes[d].astype(f32)
            return 0

        lax.fori_loop(share * j, share * (j + 1), widen, 0, unroll=8)

    size = 16
    row = lax.broadcasted_iota(jnp.int32, (size, 1), 0)

    def one(k, _):
        lanes = lanes_of(k)
        for copy in inputs(k):
            copy.wait()
        for i in range(3):
            short_ref[i, :, lanes] = ext_ref[k, TOTAL + 3 * i : TOTAL + 3 * i + 3, :]
        skip_ref[:, lanes] = ext_ref[k, TOTAL + 9 : TOTAL + 10, :]
        scales = [ext_ref[k, SCALE + slot : SCALE + slot + 1, :] for slot in range(2)]
        for slot in range(2):
            turned[slot] = wide[pl.ds(8 * slot + k, GROUPS, stride=16), :].T
        taps = [[weight_ref[i, j : j + 1, lanes] for j in range(3)] for i in range(3)]

        following = [ext_ref[k, AFTER + 2 * i : AFTER + 2 * i + 2, :] for i in range(3)]
        lead = []
        for i in range(3):
            second, final = (ext_ref[k, BEFORE + 2 * i + j : BEFORE + 2 * i + j + 1, :] for j in range(2))
            lead.append((taps[i][1] * final + taps[i][2] * second, taps[i][2] * final))
        for begin in reversed(range(0, ROWS, size)):
            rows = slice(begin, begin + size)
            conv, grad_mixer = (decode(turned[slot, rows, :], scales[slot]) for slot in range(2))
            forms = [shaped[k, i, rows, :] for i in range(3)]
            if begin == 0:
                for i in range(3):
                    forms[i] = forms[i] + jnp.where(row == 0, lead[i][0], jnp.where(row == 1, lead[i][1], 0.0))
            query, key, value = forms
            mixed[k, rows, :] = (query * conv).astype(bf16)
            slopes = (cot[k, rows, :].astype(f32) * conv, grad_mixer * value, grad_mixer * key)
            for i in range(3):
                slope, after = slopes[i], following[i]
                one = jnp.where(row == size - 1, after[0:1], pltpu.roll(slope, size - 1, 0))
                two = jnp.where(row >= size - 2, pltpu.roll(one, size - 1, 0), pltpu.roll(slope, size - 2, 0))
                two = jnp.where(row == size - 1, after[1:2], two)
                grad[k, i, rows, :] = taps[i][0] * slope + taps[i][1] * one + taps[i][2] * two
            following = [slope[:2] for slope in slopes]
        for copy in results(k):
            copy.start()
        return 0

    lax.fori_loop(0, COPIES, one, 0)
    for k in range(COPIES):
        for copy in results(k):
            copy.wait()


def exchange(values):
    return lax.all_to_all(values, "ctx", split_axis=0, concat_axis=0, tiled=True)


def pack(features, cotangent, long_filter):
    anywhere = pl.BlockSpec(memory_space=pl.ANY)
    return pl.pallas_call(
        pack_kernel,
        in_specs=[anywhere] * 3,
        out_specs=anywhere,
        out_shape=jax.ShapeDtypeStruct((BLOCKS, SEND_ROWS, ROWS), bf16),
        scratch_shapes=[
            pltpu.VMEM((COPIES, 3, ROWS, GROUPS), bf16),
            pltpu.VMEM((COPIES, ROWS, GROUPS), bf16),
            pltpu.VMEM((ROWS, GROUPS), f32),
            pltpu.VMEM((BLOCKS, SEND_ROWS, ROWS), bf16),
            pltpu.VMEM((4, COPIES * SPACING, ROWS), f32),
            pltpu.VMEM((2, GROUPS, ROWS), f32),
            pltpu.SemaphoreType.DMA((COPIES,)),
            pltpu.SemaphoreType.DMA((COPIES,)),
            pltpu.SemaphoreType.DMA,
            pltpu.SemaphoreType.DMA((4,)),
        ],
        compiler_params=ROOMY,
        name="pack",
    )(features, cotangent, long_filter)


def convolve(gathered, own):
    constants = tables()
    anywhere = pl.BlockSpec(memory_space=pl.ANY)
    whole = lambda array: pl.BlockSpec(array.shape, lambda i: (0,) * array.ndim)
    return pl.pallas_call(
        conv_kernel,
        grid=(1,),
        in_specs=[
            anywhere,
            pl.BlockSpec((BLOCKS, 2 * OWN, ROWS), lambda i: (0, SIGNAL_ROWS // (2 * OWN), 0)),
            whole(own),
        ]
        + [whole(array) for array in constants],
        out_specs=anywhere,
        out_shape=jax.ShapeDtypeStruct((BLOCKS, BACK_ROWS, ROWS), bf16),
        scratch_shapes=[
            pltpu.VMEM((OWN, BLOCKS, 4 * COPIES, ROWS), bf16),
            pltpu.VMEM((OWN + 1, BLOCKS, 2 * COPIES, ROWS), bf16),
            pltpu.SemaphoreType.DMA((OWN,)),
            pltpu.SemaphoreType.DMA((OWN + 1,)),
            pltpu.VMEM((2, COPIES * BLOCKS, ROWS), f32),
            pltpu.VMEM((2, COPIES * BLOCKS, ROWS), f32),
            pltpu.VMEM((2, BLOCKS, 24, ROWS), f32),
            pltpu.VMEM((2, BLOCKS, 24, ROWS), f32),
            pltpu.VMEM((2, BLOCKS, 24, ROWS), f32),
            pltpu.VMEM((2 * COPIES * LINES, 2 * ROWS), bf16),
            pltpu.VMEM((2 * COPIES * LINES, 2 * ROWS), bf16),
            pltpu.VMEM((2 * COPIES * LINES, 2 * ROWS), f32),
            pltpu.VMEM((OWN, LINES, 2 * ROWS), f32),
            pltpu.VMEM((OWN, LINES, 2 * ROWS), f32),
            pltpu.VMEM((BLOCKS + 1, COPIES, ROWS), f32),
            pltpu.VMEM((BLOCKS, COPIES, ROWS), f32),
            pltpu.VMEM((2 * OWN * BLOCKS, ROWS), f32),
            pltpu.VMEM((OWN, COPIES, ROWS), f32),
            pltpu.VMEM((COPIES * BLOCKS, ROWS), f32),
            pltpu.VMEM((COPIES * BLOCKS, ROWS), f32),
        ],
        compiler_params=LIMIT,
        name="conv",
    )(gathered, gathered, own, *constants)


def unpack_extras(home):
    spread = np.zeros((OWN, BLOCKS, GROUPS), ml_dtypes.bfloat16)
    for gi in range(OWN):
        spread[gi, np.arange(BLOCKS), OWN * np.arange(BLOCKS) + gi] = 1.0
    return pl.pallas_call(
        extras_kernel,
        grid=(1,),
        in_specs=[
            pl.BlockSpec((BLOCKS, 2 * COPIES, ROWS), lambda i: (0, RESULT_ROWS // (2 * COPIES), 0)),
            pl.BlockSpec((OWN, BLOCKS, GROUPS), lambda i: (0, 0, 0)),
        ],
        out_specs=[
            pl.BlockSpec((ROWS, GROUPS // 2), lambda i: (0, 0)),
            pl.BlockSpec((ROWS, GROUPS // 2), lambda i: (0, 0)),
            pl.BlockSpec((COPIES, 32, GROUPS), lambda i: (0, 0, 0)),
        ],
        out_shape=[
            jax.ShapeDtypeStruct((ROWS, GROUPS // 2), f32),
            jax.ShapeDtypeStruct((ROWS, GROUPS // 2), f32),
            jax.ShapeDtypeStruct((COPIES, 32, GROUPS), f32),
        ],
        scratch_shapes=[pltpu.VMEM((16 * BLOCKS, ROWS), f32)],
        compiler_params=LIMIT,
        name="extras",
    )(home, spread)


def prepare(features, short_weight):
    breadth = features.shape[2]
    deep = lambda k: (0, 0, k)
    width = 2 * GROUPS
    return pl.pallas_call(
        prepare_kernel,
        grid=(breadth // width,),
        in_specs=[pl.BlockSpec((3, ROWS, width), deep), pl.BlockSpec((3, 3, width), deep)],
        out_specs=pl.BlockSpec((3, ROWS, width), deep),
        out_shape=jax.ShapeDtypeStruct((3, ROWS, breadth), f32),
        compiler_params=LIMIT,
        name="prepare",
    )(features, short_weight)


def finish(home, shaped, cotangent, short_weight, ext):
    breadth = shaped.shape[2]
    anywhere = pl.BlockSpec(memory_space=pl.ANY)
    whole = lambda *shape: pl.BlockSpec(shape, lambda i: (0,) * len(shape))
    return pl.pallas_call(
        finish_kernel,
        grid=(1,),
        in_specs=[anywhere] * 3 + [whole(*array.shape) for array in (short_weight, ext)],
        out_specs=[anywhere, anywhere, whole(3, 3, breadth), whole(1, breadth)],
        out_shape=[
            jax.ShapeDtypeStruct((ROWS, breadth), bf16),
            jax.ShapeDtypeStruct((3, ROWS, breadth), f32),
            jax.ShapeDtypeStruct((3, 3, breadth), f32),
            jax.ShapeDtypeStruct((1, breadth), f32),
        ],
        scratch_shapes=[
            pltpu.VMEM((BLOCKS, RESULT_ROWS, ROWS), bf16),
            pltpu.VMEM((COPIES, 3, ROWS, GROUPS), f32),
            pltpu.VMEM((COPIES, ROWS, GROUPS), bf16),
            pltpu.VMEM((COPIES, ROWS, GROUPS), bf16),
            pltpu.VMEM((COPIES, 3, ROWS, GROUPS), f32),
            pltpu.VMEM((RESULT_ROWS * BLOCKS, ROWS), f32),
            pltpu.VMEM((2, ROWS, GROUPS), f32),
            pltpu.SemaphoreType.DMA((4,)),
        ]
        + [pltpu.SemaphoreType.DMA((COPIES,))] * 4,
        compiler_params=LIMIT,
        name="finish",
    )(home, shaped, cotangent, short_weight, ext)


def shards(features, short_weight, skip, long_filter, cotangent):
    breadth = features.shape[2]

    gathered = exchange(pack(features, cotangent, long_filter))

    weights = jnp.concatenate([short_weight.reshape(9, breadth), skip[None]], axis=0)
    weights = weights.reshape(10, COPIES, GROUPS)

    shaped = prepare(features, short_weight)

    gathered, weights, shaped = lax.optimization_barrier((gathered, weights, shaped))
    home = exchange(convolve(gathered, weights))

    mine, other, ext = unpack_extras(home)
    arrived = lax.ppermute(other, "ch", [(0, 1), (1, 0)])
    mixed, feature_gradient, grad_short, grad_skip = finish(home, shaped, cotangent, short_weight, ext)
    return (mixed, feature_gradient, grad_short, grad_skip.reshape(breadth), mine + arrived)


def solution(mesh):
    return jax.shard_map(
        shards,
        mesh=mesh,
        in_specs=(
            P(None, "ctx", "ch"),
            P(None, None, "ch"),
            P("ch"),
            P("ctx", None),
            P("ctx", "ch"),
        ),
        out_specs=(
            P("ctx", "ch"),
            P(None, "ctx", "ch"),
            P(None, None, "ch"),
            P("ch"),
            P("ctx", "ch"),
        ),
        check_vma=False,
    )
```

```python
import functools
import math

import jax
import jax.numpy as jnp
import ml_dtypes
import numpy as np
from jax import lax
from jax.experimental import pallas as pl
from jax.experimental.pallas import tpu as pltpu
from jax.sharding import PartitionSpec as P

f32 = jnp.float32
bf16 = jnp.bfloat16

BLOCKS = 64
ROWS = 128
COPIES = 8
GROUPS = 256
OWN = GROUPS // BLOCKS
LINES = 72
PERIOD = 2 * BLOCKS * ROWS
SIGNAL_ROWS = OWN * 4 * COPIES
SEND_ROWS = SIGNAL_ROWS + 2 * OWN
RESULT_ROWS = OWN * 2 * COPIES
BACK_ROWS = RESULT_ROWS + 2 * COPIES
AFTER, TOTAL, SPLIT = 0, 6, 16
BEFORE, SCALE, FILTER_SCALE = 16, 22, 24
LEVELS = 250.0
BIAS = 125.0
GANG = 8
SPACING = GROUPS + 1
LIMIT = pltpu.CompilerParams(vmem_limit_bytes=32 * 2**20)
ROOMY = pltpu.CompilerParams(vmem_limit_bytes=60 * 2**20)


def high_low(values):
    high = values.astype(ml_dtypes.bfloat16)
    low = (values - high.astype(np.float64)).astype(ml_dtypes.bfloat16)
    return high, low


def tables():
    k1 = np.arange(65)
    a = np.arange(BLOCKS)
    b = np.arange(ROWS)
    turn = 2.0 * np.pi * (k1[:, None] * a[None, :] % ROWS) / ROWS
    first = np.zeros((2 * LINES, BLOCKS))
    first[:65] = np.cos(turn)
    first[LINES : LINES + 65] = -np.sin(turn)
    weight = np.where((k1 == 0) | (k1 == 64), 1.0, 2.0)[:, None] / PERIOD
    last = np.zeros((BLOCKS, 2 * LINES))
    last[:, :65] = (weight * np.cos(turn)).T
    last[:, LINES : LINES + 65] = (-weight * np.sin(turn)).T
    twiddle = np.zeros((2, LINES, ROWS))
    twiddle[0, :65] = np.cos(2.0 * np.pi * k1[:, None] * b[None, :] / PERIOD)
    twiddle[1, :65] = np.sin(2.0 * np.pi * k1[:, None] * b[None, :] / PERIOD)
    angle = 2.0 * np.pi * (b[:, None] * b[None, :] % ROWS) / ROWS
    cosine, sine = np.cos(angle), np.sin(angle)
    forward = np.block([[cosine, -sine], [sine, cosine]])
    first_h, first_l = high_low(first)
    last_h, last_l = high_low(last)
    forward_h, forward_l = high_low(forward)
    return (
        np.concatenate([first_h, first_h, first_l], axis=1),
        np.concatenate([last_h, last_h, last_l], axis=1),
        twiddle.astype(np.float32),
        np.concatenate([forward_h, forward_h, forward_l], axis=0),
    )


def split(values):
    high = values.astype(bf16)
    return high, (values - high.astype(f32)).astype(bf16)


def dot(left, right):
    return jnp.dot(left, right, preferred_element_type=f32)


def encode(values, scale):
    code = jnp.exp2(jnp.abs(values) * (LEVELS / scale) - BIAS)
    return jnp.where(values < 0.0, -code, code)


def scale_of(largest):
    return (jnp.maximum(largest, 1e-30) * (1.0 + 1.0 / 128.0)).astype(bf16).astype(f32)


def decode(code, scale):
    step = scale * (1.0 / LEVELS)
    value = jnp.log(jnp.abs(code)) * (step * (1.0 / math.log(2.0))) + step * BIAS
    return jnp.where(code < 0.0, -value, value)


def pack_kernel(
    feat_ref, cot_ref, filt_ref, out_ref, feat, cot, filt, packed, turned, taps, feat_sem, cot_sem, filt_sem, out_sem
):
    arriving = []
    for k in range(COPIES):
        lanes = pl.ds(GROUPS * k, GROUPS)
        arriving.append(
            (
                pltpu.make_async_copy(feat_ref.at[:, :, lanes], feat.at[k], feat_sem.at[k]),
                pltpu.make_async_copy(cot_ref.at[:, lanes], cot.at[k], cot_sem.at[k]),
            )
        )
    filter_copy = pltpu.make_async_copy(filt_ref, filt, filt_sem)
    filter_copy.start()
    for copies in arriving:
        for copy in copies:
            copy.start()

    filter_copy.wait()
    value = filt[...].T
    high = value.astype(bf16).astype(f32)
    taps[0] = high
    taps[1] = value - high
    for k in range(COPIES):
        for copy in arriving[k]:
            copy.wait()
        for part in range(4):
            source = cot[k] if part == 3 else feat[k, part]
            turned[part, SPACING * k : SPACING * k + GROUPS, :] = source.astype(f32).T

    def one(d, _):
        for gi in range(OWN):
            n = OWN * d + gi
            tiles = [turned.at[part][pl.ds(n, COPIES, stride=SPACING), :] for part in range(4)]
            packed[d, 32 * gi : 32 * gi + 16, :] = jnp.concatenate(tiles[:2], axis=0).astype(bf16)
            packed[d, 32 * gi + 16 : 32 * gi + 32, :] = jnp.concatenate(tiles[2:], axis=0).astype(bf16)
        pieces = [taps[part, pl.ds(OWN * d, OWN), :] for part in range(2)]
        packed[d, SIGNAL_ROWS:SEND_ROWS, :] = jnp.concatenate(pieces, axis=0).astype(bf16)
        return 0

    leaving = []
    share = BLOCKS // 4
    for j in range(4):
        lax.fori_loop(share * j, share * (j + 1), one, 0, unroll=4)
        place = pl.ds(share * j, share)
        leaving.append(pltpu.make_async_copy(packed.at[place], out_ref.at[place], out_sem.at[j]))
        leaving[-1].start()
    for copy in leaving:
        copy.wait()


def conv_kernel(
    in_ref, taps_ref, weight_ref, first_ref, last_ref, twiddle_ref, forward_ref, out_ref,
    raw_buf, code_buf, in_sem, out_sem,
    left, right, shift_one, shift_two, formed, spec_high, spec_low, lines, filt, cross, extra, exact, taps, totals, own, own_scale,
):
    chunk = 8
    steps = BLOCKS // chunk
    lane = lax.broadcasted_iota(jnp.int32, (1, 1, ROWS), 2)
    flat = lane[0]
    cosine, sine = twiddle_ref[0], twiddle_ref[1]

    def arriving(gi):
        rows = pl.ds(pl.multiple_of(4 * COPIES * gi, 4 * COPIES), 4 * COPIES)
        return pltpu.make_async_copy(in_ref.at[:, rows, :], raw_buf.at[gi], in_sem.at[gi])

    def leaving(gi):
        rows = pl.ds(pl.multiple_of(2 * COPIES * gi, 2 * COPIES), 2 * COPIES)
        return pltpu.make_async_copy(code_buf.at[gi], out_ref.at[:, rows, :], out_sem.at[gi])

    for gi in range(OWN):
        arriving(gi).start()

    rank = lax.axis_index("ctx")
    column = lax.broadcasted_iota(jnp.int32, (1, GROUPS), 1)
    own_weights = []
    for gi in range(OWN):
        mine = column == OWN * rank + gi
        own_weights.append(
            [jnp.sum(jnp.where(mine, weight_ref[i], 0.0), axis=1, keepdims=True) for i in range(10)]
        )

    def tile_rows(a0):
        return pl.ds(pl.multiple_of(COPIES * a0, 64), COPIES * chunk)

    def shape(weights, signals):
        shaped = []
        for i in range(3):
            rows = slice(8 * i, 8 * i + 8)
            shaped.append(sum(weights[3 * i + j] * signals[j][:, rows] for j in range(3)))
        return shaped

    def pick(ref, k):
        return ref[pl.ds(k, BLOCKS, stride=COPIES), :]

    def to_lines(blocks, base):
        both = jnp.concatenate(blocks, axis=1)
        high, low = split(both)
        mid = dot(first_ref[...], jnp.concatenate([high, low, high], axis=0))
        out = []
        for j in range(2):
            real = mid[:LINES, ROWS * j : ROWS * (j + 1)]
            imag = mid[LINES:, ROWS * j : ROWS * (j + 1)]
            out.append(jnp.concatenate([real * cosine + imag * sine, imag * cosine - real * sine], axis=1))
        keep(jnp.concatenate(out, axis=0), base)

    def keep(values, base):
        high, low = split(values)
        spec_high[base : base + 2 * LINES, :] = high
        spec_low[base : base + 2 * LINES, :] = low

    def over_rows(begin, count):
        rows = slice(LINES * begin, LINES * (begin + count))
        high = spec_high[rows, :]
        return dot(jnp.concatenate([high, spec_low[rows, :], high], axis=1), forward_ref[...])

    def from_lines(values):
        pieces = []
        for j in range(2):
            imag = values[LINES * j : LINES * (j + 1), :ROWS]
            real = values[LINES * j : LINES * (j + 1), ROWS:]
            pieces.append(jnp.concatenate([real * cosine - imag * sine, imag * cosine + real * sine], axis=0))
        high, low = split(jnp.concatenate(pieces, axis=1))
        both = dot(last_ref[...], jnp.concatenate([high, low, high], axis=0))
        return both[:, :ROWS], both[:, ROWS:]

    def spin(values, amount):
        return pltpu.roll(values, amount, values.ndim - 1) if amount else values

    def shape_steps(gi):
        weights = own_weights[gi]
        carry = [jnp.zeros((24, ROWS), f32)] * 2
        mix, grad, ones, twos, forms = (ref.at[gi % 2] for ref in (left, right, shift_one, shift_two, formed))

        def step(a0):
            if a0 == 0:
                arriving(gi).wait()
            raw = raw_buf[gi, a0 : a0 + chunk].astype(f32)
            signal = raw[:, :24]
            one = pltpu.roll(signal, 1, 2)
            two = pltpu.roll(signal, 2, 2)
            one_before = jnp.concatenate([carry[0][None], one[:-1]], axis=0)
            two_before = jnp.concatenate([carry[1][None], two[:-1]], axis=0)
            delayed = (jnp.where(lane < 1, one_before, one), jnp.where(lane < 2, two_before, two))
            ones[a0 : a0 + chunk] = delayed[0]
            twos[a0 : a0 + chunk] = delayed[1]
            shaped = shape(weights, (signal,) + delayed)
            forms[a0 : a0 + chunk] = jnp.concatenate(shaped, axis=1)
            rows = slice(COPIES * a0, COPIES * (a0 + chunk))
            mix[rows, :] = (shaped[1] * shaped[2]).reshape(COPIES * chunk, ROWS)
            grad[rows, :] = (raw[:, 24:] * shaped[0]).reshape(COPIES * chunk, ROWS)
            carry[:] = [one[-1], two[-1]]

        return [functools.partial(step, a0) for a0 in range(0, BLOCKS, chunk)]

    def finish_steps(gi):
        weights = own_weights[gi]
        sums = [jnp.zeros((COPIES, ROWS), f32)] * 10
        mix, grad, ones, twos, forms = (ref.at[gi % 2] for ref in (left, right, shift_one, shift_two, formed))

        def step(a0):
            rows = slice(COPIES * a0, COPIES * (a0 + chunk))
            raw = raw_buf[gi, a0 : a0 + chunk].astype(f32)
            upstream = raw[:, 24:]
            signals = (raw[:, :24], ones[a0 : a0 + chunk], twos[a0 : a0 + chunk])
            shaped = [forms[a0 : a0 + chunk, 8 * i : 8 * i + 8] for i in range(3)]
            mixer = shaped[1] * shaped[2]
            grad_conv = upstream * shaped[0]
            conv = mix[rows, :].reshape(chunk, COPIES, ROWS) + weights[9] * mixer
            grad_mixer = grad[rows, :].reshape(chunk, COPIES, ROWS) + weights[9] * grad_conv
            grads = (upstream * conv, grad_mixer * shaped[2], grad_mixer * shaped[1])
            for i in range(3):
                for j in range(3):
                    sums[3 * i + j] += jnp.sum(grads[i] * signals[j][:, 8 * i : 8 * i + 8], axis=0)
            sums[9] += jnp.sum(grad_conv * mixer, axis=0)

            codes = []
            entry = jnp.zeros((COPIES, ROWS), f32)
            for slot, value in ((0, conv), (1, grad_mixer)):
                scale = scale_of(jnp.max(jnp.max(jnp.abs(value), axis=0), axis=1, keepdims=True))
                codes.append(encode(value, scale).astype(bf16))
                entry = entry + jnp.where(flat == 32 * gi + SCALE + slot, scale, 0.0)
            code_buf[gi, a0 : a0 + chunk] = jnp.concatenate(codes, axis=1)
            ahead = jnp.zeros((chunk, COPIES, ROWS), f32)
            behind = jnp.broadcast_to(entry, (chunk, COPIES, ROWS))
            for i in range(3):
                place = 32 * gi + AFTER + 2 * i
                ahead = jnp.where((lane >= place) & (lane < place + 2), spin(grads[i], place), ahead)
                place = 32 * gi + BEFORE + 2 * i
                moved = spin(signals[2][:, 8 * i : 8 * i + 8], place)
                behind = jnp.where((lane >= place) & (lane < place + 2), moved, behind)
            here = slice(a0, a0 + chunk)
            extra[here] = ahead if gi == 0 else extra[here] + ahead
            exact[here] = behind if gi == 0 else exact[here] + behind
            if a0 + chunk == BLOCKS:
                leaving(gi).start()
                total = jnp.zeros((COPIES, ROWS), f32)
                for i in range(10):
                    value = jnp.sum(sums[i], axis=1, keepdims=True) * (1.0 / math.sqrt(BLOCKS * ROWS))
                    total = total + jnp.where(flat == 32 * gi + TOTAL + i, value, 0.0)
                totals[gi] = total

        return [functools.partial(step, a0) for a0 in range(0, BLOCKS, chunk)]

    def take(steps):
        if steps:
            steps.pop(0)()

    def main(gi, before, after):
        mix, grad = left.at[gi % 2], right.at[gi % 2]
        for base, ref in ((0, mix), (COPIES, grad)):
            for k in range(0, COPIES, GANG):
                for j in range(k, k + GANG, 2):
                    to_lines([pick(ref, j), pick(ref, j + 1)], LINES * (base + j))
                    take(before)
                lines[LINES * (base + k) : LINES * (base + k + GANG), :] = over_rows(base + k, GANG)

        filt_real, filt_imag = filt[gi, :, :ROWS], filt[gi, :, ROWS:]
        cross_real = jnp.zeros((LINES, ROWS), f32)
        cross_imag = jnp.zeros((LINES, ROWS), f32)
        for pair in range(COPIES // 2):
            forth, back = [], []
            for k in (2 * pair, 2 * pair + 1):
                here = slice(LINES * k, LINES * (k + 1))
                there = slice(LINES * (COPIES + k), LINES * (COPIES + k + 1))
                mix_real, mix_imag = lines[here, :ROWS], lines[here, ROWS:]
                grad_real, grad_imag = lines[there, :ROWS], lines[there, ROWS:]
                forth.append(
                    jnp.concatenate(
                        [mix_real * filt_imag + mix_imag * filt_real, mix_real * filt_real - mix_imag * filt_imag], axis=1
                    )
                )
                back.append(
                    jnp.concatenate(
                        [
                            grad_imag * filt_real - grad_real * filt_imag,
                            grad_real * filt_real + grad_imag * filt_imag,
                        ],
                        axis=1,
                    )
                )
                cross_real = cross_real + grad_real * mix_real + grad_imag * mix_imag
                cross_imag = cross_imag + grad_imag * mix_real - grad_real * mix_imag
            keep(jnp.concatenate(forth, axis=0), 2 * LINES * pair)
            keep(jnp.concatenate(back, axis=0), 2 * LINES * (COPIES // 2 + pair))
        cross[gi] = jnp.concatenate([cross_imag, cross_real], axis=1)
        for k in range(0, COPIES, GANG):
            for target, base in ((mix, 0), (grad, COPIES)):
                values = over_rows(base + k, GANG)
                for j in range(0, GANG, 2):
                    pair = from_lines(values[LINES * j : LINES * (j + 2), :])
                    for i in range(2):
                        target[pl.ds(k + j + i, BLOCKS, stride=COPIES), :] = pair[i]
                    take(after)

    def filter_gradient():
        for f in range(0, OWN, 2):
            keep(cross[f : f + 2].reshape(2 * LINES, 2 * ROWS), LINES * f)
        temporal = over_rows(0, OWN)
        scale = 1.0 / math.sqrt(BLOCKS * ROWS * 2 * COPIES)
        values = []
        for f in range(0, OWN, 2):
            values.extend(from_lines(temporal[LINES * f : LINES * (f + 2)]))
        codes = []
        scales = jnp.zeros((BLOCKS, ROWS), f32)
        for f in range(OWN):
            value = values[f] * scale
            size = scale_of(jnp.max(jnp.abs(value), axis=1, keepdims=True))
            codes.append(encode(value, size))
            scales = jnp.where(flat == 32 * f + FILTER_SCALE, size, scales)
        for k in range(COPIES):
            moved = jnp.zeros((BLOCKS, ROWS), f32)
            for f in range(OWN):
                inside = (flat >= 32 * f + SPLIT) & (flat < 32 * f + 32)
                moved = jnp.where(inside, spin(codes[f], (32 * f + SPLIT - 16 * k) % ROWS), moved)
            own[pl.ds(k, BLOCKS, stride=COPIES), :] = moved
            own_scale[pl.ds(k, BLOCKS, stride=COPIES), :] = scales

    def wrap_up():
        every = totals[0] + totals[1] + totals[2] + totals[3]

        def write(step, _):
            a0 = chunk * step
            value = extra[pl.ds(a0 + 1, chunk)] + every[None]
            high = value.astype(bf16).astype(f32)
            code = own[tile_rows(a0), :].reshape(chunk, COPIES, ROWS)
            single = exact[pl.ds(a0, chunk)] + own_scale[tile_rows(a0), :].reshape(chunk, COPIES, ROWS)
            both = [jnp.where(lane % 32 < SPLIT, high, code), jnp.where(lane % 32 < SPLIT, value - high, single)]
            code_buf[OWN, pl.ds(a0, chunk)] = jnp.concatenate(both, axis=1).astype(bf16)
            return 0

        lax.fori_loop(0, steps, write, 0, unroll=8)

    def widen(a, _):
        taps[pl.ds(pl.multiple_of(2 * OWN * a, 2 * OWN), 2 * OWN), :] = taps_ref[a].astype(f32)
        return 0

    lax.fori_loop(0, BLOCKS, widen, 0, unroll=8)
    blocks = []
    for f in range(OWN):
        parts = [taps[pl.ds(OWN * part + f, BLOCKS, stride=2 * OWN), :] for part in range(2)]
        blocks.append(parts[0] + parts[1])
    for f in range(0, OWN, 2):
        to_lines(blocks[f : f + 2], LINES * f)
    filt[...] = over_rows(0, OWN).reshape(OWN, LINES, 2 * ROWS)
    extra[BLOCKS] = jnp.zeros((COPIES, ROWS), f32)
    for step in shape_steps(0):
        step()
    before = []
    for gi in range(OWN):
        after = shape_steps(gi + 1) if gi + 1 < OWN else []
        main(gi, before, after)
        before = finish_steps(gi)
    filter_gradient()
    for step in before:
        step()
    wrap_up()
    leaving(OWN).start()
    for gi in range(OWN + 1):
        leaving(gi).wait()


def extras_kernel(in_ref, spread_ref, mine_ref, other_ref, ext_ref, wide):
    half = lax.axis_index("ch")

    def widen(d, _):
        wide[pl.ds(pl.multiple_of(16 * d, 16), 16), :] = in_ref[d].astype(f32)
        return 0

    lax.fori_loop(0, BLOCKS, widen, 0, unroll=8)
    turned = [wide[pl.ds(n, BLOCKS, stride=16), :].T.astype(bf16) for n in range(2 * COPIES)]
    total = jnp.zeros((2 * COPIES * 32, GROUPS), f32)
    for gi in range(OWN):
        rows = slice(32 * gi, 32 * gi + 32)
        total = total + dot(jnp.concatenate([piece[rows] for piece in turned], axis=0), spread_ref[gi])
    for k in range(COPIES):
        first = total[32 * k : 32 * k + 32]
        second = total[32 * (COPIES + k) : 32 * (COPIES + k) + 32]
        value = decode(first[SPLIT:], second[FILTER_SCALE : FILTER_SCALE + 1])
        low, high = value[:, : GROUPS // 2], value[:, GROUPS // 2 :]
        mine_ref[16 * k : 16 * (k + 1), :] = jnp.where(half == 0, low, high)
        other_ref[16 * k : 16 * (k + 1), :] = jnp.where(half == 0, high, low)
        ext_ref[k, :SPLIT, :] = first[:SPLIT] + second[:SPLIT]
        ext_ref[k, SPLIT:, :] = second[SPLIT:]


def prepare_kernel(feat_ref, weight_ref, out_ref):
    row = lax.broadcasted_iota(jnp.int32, (ROWS, 1), 0)
    for i in range(3):
        value = feat_ref[i].astype(f32)
        one = jnp.where(row < 1, 0.0, pltpu.roll(value, 1, 0))
        two = jnp.where(row < 2, 0.0, pltpu.roll(value, 2, 0))
        out_ref[i] = weight_ref[i, 0:1, :] * value + weight_ref[i, 1:2, :] * one + weight_ref[i, 2:3, :] * two


def finish_kernel(
    in_ref, shaped_ref, cot_ref, weight_ref, ext_ref, mixed_ref, grad_ref, short_ref, skip_ref,
    mixed, grad, wide, turned, mixed_sem, grad_sem,
):
    def lanes_of(k):
        return pl.ds(pl.multiple_of(GROUPS * k, GROUPS), GROUPS)

    def wide_lanes(k):
        return pl.ds(pl.multiple_of(2 * GROUPS * k, 2 * GROUPS), 2 * GROUPS)

    def results(k):
        return (
            pltpu.make_async_copy(mixed.at[k], mixed_ref.at[:, wide_lanes(k)], mixed_sem.at[k]),
            pltpu.make_async_copy(grad.at[k], grad_ref.at[:, :, wide_lanes(k)], grad_sem.at[k]),
        )

    def widen(d, _):
        place = pl.ds(pl.multiple_of(RESULT_ROWS * d, RESULT_ROWS), RESULT_ROWS)
        wide[place, :] = in_ref[d, :RESULT_ROWS, :].astype(f32)
        return 0

    lax.fori_loop(0, BLOCKS, widen, 0, unroll=8)

    size = 16
    row = lax.broadcasted_iota(jnp.int32, (size, 1), 0)

    def one(k0, _):
        for part in range(2):
            half(k0, part)
        for copy in results(k0):
            copy.start()
        return 0

    def half(k0, part):
        k = 2 * k0 + part
        lanes = lanes_of(k)
        spot = slice(GROUPS * part, GROUPS * (part + 1))
        for i in range(3):
            short_ref[i, :, lanes] = ext_ref[k, TOTAL + 3 * i : TOTAL + 3 * i + 3, :]
        skip_ref[:, lanes] = ext_ref[k, TOTAL + 9 : TOTAL + 10, :]
        scales = [ext_ref[k, SCALE + slot : SCALE + slot + 1, :] for slot in range(2)]
        for slot in range(2):
            turned[slot] = wide[pl.ds(8 * slot + k, GROUPS, stride=16), :].T
        taps = [[weight_ref[i, j : j + 1, lanes] for j in range(3)] for i in range(3)]

        following = [ext_ref[k, AFTER + 2 * i : AFTER + 2 * i + 2, :] for i in range(3)]
        lead = []
        for i in range(3):
            second, final = (ext_ref[k, BEFORE + 2 * i + j : BEFORE + 2 * i + j + 1, :] for j in range(2))
            lead.append((taps[i][1] * final + taps[i][2] * second, taps[i][2] * final))
        for begin in reversed(range(0, ROWS, size)):
            rows = slice(begin, begin + size)
            conv, grad_mixer = (decode(turned[slot, rows, :], scales[slot]) for slot in range(2))
            forms = [shaped_ref[i, rows, lanes] for i in range(3)]
            if begin == 0:
                for i in range(3):
                    forms[i] = forms[i] + jnp.where(row == 0, lead[i][0], jnp.where(row == 1, lead[i][1], 0.0))
            query, key, value = forms
            mixed[k0, rows, spot] = (query * conv).astype(bf16)
            slopes = (cot_ref[rows, lanes].astype(f32) * conv, grad_mixer * value, grad_mixer * key)
            for i in range(3):
                slope, after = slopes[i], following[i]
                one = jnp.where(row == size - 1, after[0:1], pltpu.roll(slope, size - 1, 0))
                two = jnp.where(row >= size - 2, pltpu.roll(one, size - 1, 0), pltpu.roll(slope, size - 2, 0))
                two = jnp.where(row == size - 1, after[1:2], two)
                grad[k0, i, rows, spot] = taps[i][0] * slope + taps[i][1] * one + taps[i][2] * two
            following = [slope[:2] for slope in slopes]

    lax.fori_loop(0, COPIES // 2, one, 0)
    for k in range(COPIES // 2):
        for copy in results(k):
            copy.wait()


def exchange(values):
    return lax.all_to_all(values, "ctx", split_axis=0, concat_axis=0, tiled=True)


def pack(features, cotangent, long_filter):
    anywhere = pl.BlockSpec(memory_space=pl.ANY)
    return pl.pallas_call(
        pack_kernel,
        in_specs=[anywhere] * 3,
        out_specs=anywhere,
        out_shape=jax.ShapeDtypeStruct((BLOCKS, SEND_ROWS, ROWS), bf16),
        scratch_shapes=[
            pltpu.VMEM((COPIES, 3, ROWS, GROUPS), bf16),
            pltpu.VMEM((COPIES, ROWS, GROUPS), bf16),
            pltpu.VMEM((ROWS, GROUPS), f32),
            pltpu.VMEM((BLOCKS, SEND_ROWS, ROWS), bf16),
            pltpu.VMEM((4, (COPIES + 1) * SPACING, ROWS), f32),
            pltpu.VMEM((2, GROUPS, ROWS), f32),
            pltpu.SemaphoreType.DMA((COPIES,)),
            pltpu.SemaphoreType.DMA((COPIES,)),
            pltpu.SemaphoreType.DMA,
            pltpu.SemaphoreType.DMA((4,)),
        ],
        compiler_params=ROOMY,
        name="pack",
    )(features, cotangent, long_filter)


def convolve(gathered, own):
    constants = tables()
    anywhere = pl.BlockSpec(memory_space=pl.ANY)
    whole = lambda array: pl.BlockSpec(array.shape, lambda i: (0,) * array.ndim)
    return pl.pallas_call(
        conv_kernel,
        grid=(1,),
        in_specs=[
            anywhere,
            pl.BlockSpec((BLOCKS, 2 * OWN, ROWS), lambda i: (0, SIGNAL_ROWS // (2 * OWN), 0)),
            whole(own),
        ]
        + [whole(array) for array in constants],
        out_specs=anywhere,
        out_shape=jax.ShapeDtypeStruct((BLOCKS, BACK_ROWS, ROWS), bf16),
        scratch_shapes=[
            pltpu.VMEM((OWN, BLOCKS, 4 * COPIES, ROWS), bf16),
            pltpu.VMEM((OWN + 1, BLOCKS, 2 * COPIES, ROWS), bf16),
            pltpu.SemaphoreType.DMA((OWN,)),
            pltpu.SemaphoreType.DMA((OWN + 1,)),
            pltpu.VMEM((2, COPIES * (BLOCKS + 1), ROWS), f32),
            pltpu.VMEM((2, COPIES * (BLOCKS + 1), ROWS), f32),
            pltpu.VMEM((2, BLOCKS, 24, ROWS), f32),
            pltpu.VMEM((2, BLOCKS, 24, ROWS), f32),
            pltpu.VMEM((2, BLOCKS, 24, ROWS), f32),
            pltpu.VMEM((2 * COPIES * LINES, 2 * ROWS), bf16),
            pltpu.VMEM((2 * COPIES * LINES, 2 * ROWS), bf16),
            pltpu.VMEM((2 * COPIES * LINES, 2 * ROWS), f32),
            pltpu.VMEM((OWN, LINES, 2 * ROWS), f32),
            pltpu.VMEM((OWN, LINES, 2 * ROWS), f32),
            pltpu.VMEM((BLOCKS + 1, COPIES, ROWS), f32),
            pltpu.VMEM((BLOCKS, COPIES, ROWS), f32),
            pltpu.VMEM((2 * OWN * (BLOCKS + 1), ROWS), f32),
            pltpu.VMEM((OWN, COPIES, ROWS), f32),
            pltpu.VMEM((COPIES * (BLOCKS + 1), ROWS), f32),
            pltpu.VMEM((COPIES * (BLOCKS + 1), ROWS), f32),
        ],
        compiler_params=LIMIT,
        name="conv",
    )(gathered, gathered, own, *constants)


def unpack_extras(home):
    spread = np.zeros((OWN, BLOCKS, GROUPS), ml_dtypes.bfloat16)
    for gi in range(OWN):
        spread[gi, np.arange(BLOCKS), OWN * np.arange(BLOCKS) + gi] = 1.0
    return pl.pallas_call(
        extras_kernel,
        grid=(1,),
        in_specs=[
            pl.BlockSpec((BLOCKS, 2 * COPIES, ROWS), lambda i: (0, RESULT_ROWS // (2 * COPIES), 0)),
            pl.BlockSpec((OWN, BLOCKS, GROUPS), lambda i: (0, 0, 0)),
        ],
        out_specs=[
            pl.BlockSpec((ROWS, GROUPS // 2), lambda i: (0, 0)),
            pl.BlockSpec((ROWS, GROUPS // 2), lambda i: (0, 0)),
            pl.BlockSpec((COPIES, 32, GROUPS), lambda i: (0, 0, 0)),
        ],
        out_shape=[
            jax.ShapeDtypeStruct((ROWS, GROUPS // 2), f32),
            jax.ShapeDtypeStruct((ROWS, GROUPS // 2), f32),
            jax.ShapeDtypeStruct((COPIES, 32, GROUPS), f32),
        ],
        scratch_shapes=[pltpu.VMEM((16 * (BLOCKS + 1), ROWS), f32)],
        compiler_params=LIMIT,
        name="extras",
    )(home, spread)


def prepare(features, short_weight):
    breadth = features.shape[2]
    deep = lambda k: (0, 0, k)
    width = 2 * GROUPS
    return pl.pallas_call(
        prepare_kernel,
        grid=(breadth // width,),
        in_specs=[pl.BlockSpec((3, ROWS, width), deep), pl.BlockSpec((3, 3, width), deep)],
        out_specs=pl.BlockSpec((3, ROWS, width), deep),
        out_shape=jax.ShapeDtypeStruct((3, ROWS, breadth), f32),
        compiler_params=LIMIT,
        name="prepare",
    )(features, short_weight)


def finish(home, shaped, cotangent, short_weight, ext):
    breadth = shaped.shape[2]
    anywhere = pl.BlockSpec(memory_space=pl.ANY)
    vmem = pl.BlockSpec(memory_space=pltpu.VMEM)
    return pl.pallas_call(
        finish_kernel,
        in_specs=[vmem] * 5,
        out_specs=[anywhere, anywhere, vmem, vmem],
        out_shape=[
            jax.ShapeDtypeStruct((ROWS, breadth), bf16),
            jax.ShapeDtypeStruct((3, ROWS, breadth), f32),
            jax.ShapeDtypeStruct((3, 3, breadth), f32),
            jax.ShapeDtypeStruct((1, breadth), f32),
        ],
        scratch_shapes=[
            pltpu.VMEM((COPIES // 2, ROWS, 2 * GROUPS), bf16),
            pltpu.VMEM((COPIES // 2, 3, ROWS, 2 * GROUPS), f32),
            pltpu.VMEM((RESULT_ROWS * BLOCKS + 16, ROWS), f32),
            pltpu.VMEM((2, ROWS, GROUPS), f32),
            pltpu.SemaphoreType.DMA((COPIES,)),
            pltpu.SemaphoreType.DMA((COPIES,)),
        ],
        compiler_params=LIMIT,
        name="finish",
    )(home, shaped, cotangent, short_weight, ext)


def shards(features, short_weight, skip, long_filter, cotangent):
    breadth = features.shape[2]

    gathered = exchange(pack(features, cotangent, long_filter))

    weights = jnp.concatenate([short_weight.reshape(9, breadth), skip[None]], axis=0)
    weights = weights.reshape(10, COPIES, GROUPS)

    shaped = prepare(features, short_weight)

    gathered, weights, shaped = lax.optimization_barrier((gathered, weights, shaped))
    home = exchange(convolve(gathered, weights))

    mine, other, ext = unpack_extras(home)
    arrived = lax.ppermute(other, "ch", [(0, 1), (1, 0)])
    mixed, feature_gradient, grad_short, grad_skip = finish(home, shaped, cotangent, short_weight, ext)
    return (mixed, feature_gradient, grad_short, grad_skip.reshape(breadth), mine + arrived)


def solution(mesh):
    return jax.shard_map(
        shards,
        mesh=mesh,
        in_specs=(
            P(None, "ctx", "ch"),
            P(None, None, "ch"),
            P("ch"),
            P("ctx", None),
            P("ctx", "ch"),
        ),
        out_specs=(
            P("ctx", "ch"),
            P(None, "ctx", "ch"),
            P(None, None, "ch"),
            P("ch"),
            P("ctx", "ch"),
        ),
        check_vma=False,
    )
```

```python
import functools
import math

import jax
import jax.numpy as jnp
import ml_dtypes
import numpy as np
from jax import lax
from jax.experimental import pallas as pl
from jax.experimental.pallas import tpu as pltpu
from jax.sharding import PartitionSpec as P

f32 = jnp.float32
bf16 = jnp.bfloat16

BLOCKS = 64
ROWS = 128
COPIES = 8
GROUPS = 256
OWN = GROUPS // BLOCKS
LINES = 72
PERIOD = 2 * BLOCKS * ROWS
SIGNAL_ROWS = OWN * 4 * COPIES
SEND_ROWS = SIGNAL_ROWS + 2 * OWN
RESULT_ROWS = OWN * 2 * COPIES
BACK_ROWS = RESULT_ROWS + 2 * COPIES
AFTER, TOTAL, SPLIT = 0, 6, 16
BEFORE, SCALE, FILTER_SCALE = 16, 22, 24
LEVELS = 250.0
BIAS = 125.0
GANG = 8
SPACING = GROUPS + 1
LIMIT = pltpu.CompilerParams(vmem_limit_bytes=32 * 2**20)
ROOMY = pltpu.CompilerParams(vmem_limit_bytes=60 * 2**20)


def high_low(values):
    high = values.astype(ml_dtypes.bfloat16)
    low = (values - high.astype(np.float64)).astype(ml_dtypes.bfloat16)
    return high, low


def tables():
    k1 = np.arange(65)
    a = np.arange(BLOCKS)
    b = np.arange(ROWS)
    turn = 2.0 * np.pi * (k1[:, None] * a[None, :] % ROWS) / ROWS
    first = np.zeros((2 * LINES, BLOCKS))
    first[:65] = np.cos(turn)
    first[LINES : LINES + 65] = -np.sin(turn)
    weight = np.where((k1 == 0) | (k1 == 64), 1.0, 2.0)[:, None] / PERIOD
    last = np.zeros((BLOCKS, 2 * LINES))
    last[:, :65] = (weight * np.cos(turn)).T
    last[:, LINES : LINES + 65] = (-weight * np.sin(turn)).T
    twiddle = np.zeros((2, LINES, ROWS))
    twiddle[0, :65] = np.cos(2.0 * np.pi * k1[:, None] * b[None, :] / PERIOD)
    twiddle[1, :65] = np.sin(2.0 * np.pi * k1[:, None] * b[None, :] / PERIOD)
    angle = 2.0 * np.pi * (b[:, None] * b[None, :] % ROWS) / ROWS
    cosine, sine = np.cos(angle), np.sin(angle)
    forward = np.block([[cosine, -sine], [sine, cosine]])
    first_h, first_l = high_low(first)
    last_h, last_l = high_low(last)
    forward_h, forward_l = high_low(forward)
    return (
        np.concatenate([first_h, first_h, first_l], axis=1),
        np.concatenate([last_h, last_h, last_l], axis=1),
        twiddle.astype(np.float32),
        np.concatenate([forward_h, forward_h, forward_l], axis=0),
    )


def split(values):
    high = values.astype(bf16)
    return high, (values - high.astype(f32)).astype(bf16)


def dot(left, right):
    return jnp.dot(left, right, preferred_element_type=f32)


def encode(values, scale):
    code = jnp.exp2(jnp.abs(values) * (LEVELS / scale) - BIAS)
    return jnp.where(values < 0.0, -code, code)


def scale_of(largest):
    return (jnp.maximum(largest, 1e-30) * (1.0 + 1.0 / 128.0)).astype(bf16).astype(f32)


def decode(code, scale):
    step = scale * (1.0 / LEVELS)
    value = jnp.log(jnp.abs(code)) * (step * (1.0 / math.log(2.0))) + step * BIAS
    return jnp.where(code < 0.0, -value, value)


def pack_kernel(
    feat_ref, cot_ref, filt_ref, out_ref, feat, cot, filt, packed, turned, taps, feat_sem, cot_sem, filt_sem, out_sem
):
    arriving = []
    for k in range(COPIES):
        lanes = pl.ds(GROUPS * k, GROUPS)
        arriving.append(
            (
                pltpu.make_async_copy(feat_ref.at[:, :, lanes], feat.at[k], feat_sem.at[k]),
                pltpu.make_async_copy(cot_ref.at[:, lanes], cot.at[k], cot_sem.at[k]),
            )
        )
    filter_copy = pltpu.make_async_copy(filt_ref, filt, filt_sem)
    filter_copy.start()
    for copies in arriving:
        for copy in copies:
            copy.start()

    filter_copy.wait()
    value = filt[...].T
    high = value.astype(bf16).astype(f32)
    taps[0] = high
    taps[1] = value - high
    for k in range(COPIES):
        for copy in arriving[k]:
            copy.wait()
        for part in range(4):
            source = cot[k] if part == 3 else feat[k, part]
            turned[part, SPACING * k : SPACING * k + GROUPS, :] = source.T.astype(f32)

    def one(d, _):
        for gi in range(OWN):
            n = OWN * d + gi
            tiles = [turned.at[part][pl.ds(n, COPIES, stride=SPACING), :] for part in range(4)]
            packed[d, 32 * gi : 32 * gi + 16, :] = jnp.concatenate(tiles[:2], axis=0).astype(bf16)
            packed[d, 32 * gi + 16 : 32 * gi + 32, :] = jnp.concatenate(tiles[2:], axis=0).astype(bf16)
        pieces = [taps[part, pl.ds(OWN * d, OWN), :] for part in range(2)]
        packed[d, SIGNAL_ROWS:SEND_ROWS, :] = jnp.concatenate(pieces, axis=0).astype(bf16)
        return 0

    leaving = []
    share = BLOCKS // 4
    for j in range(4):
        lax.fori_loop(share * j, share * (j + 1), one, 0, unroll=4)
        place = pl.ds(share * j, share)
        leaving.append(pltpu.make_async_copy(packed.at[place], out_ref.at[place], out_sem.at[j]))
        leaving[-1].start()
    for copy in leaving:
        copy.wait()


def conv_kernel(
    in_ref, taps_ref, weight_ref, first_ref, last_ref, twiddle_ref, forward_ref, out_ref,
    raw_buf, code_buf, in_sem, out_sem,
    left, right, shift_one, shift_two, formed, spec_high, spec_low, lines, filt, cross, extra, exact, taps, totals, own, own_scale,
):
    chunk = 8
    steps = BLOCKS // chunk
    lane = lax.broadcasted_iota(jnp.int32, (1, 1, ROWS), 2)
    flat = lane[0]
    cosine, sine = twiddle_ref[0], twiddle_ref[1]

    def arriving(gi):
        rows = pl.ds(pl.multiple_of(4 * COPIES * gi, 4 * COPIES), 4 * COPIES)
        return pltpu.make_async_copy(in_ref.at[:, rows, :], raw_buf.at[gi], in_sem.at[gi])

    def leaving(gi):
        rows = pl.ds(pl.multiple_of(2 * COPIES * gi, 2 * COPIES), 2 * COPIES)
        return pltpu.make_async_copy(code_buf.at[gi], out_ref.at[:, rows, :], out_sem.at[gi])

    for gi in range(OWN):
        arriving(gi).start()

    rank = lax.axis_index("ctx")
    column = lax.broadcasted_iota(jnp.int32, (1, GROUPS), 1)
    own_weights = []
    for gi in range(OWN):
        mine = column == OWN * rank + gi
        own_weights.append(
            [jnp.sum(jnp.where(mine, weight_ref[i], 0.0), axis=1, keepdims=True) for i in range(10)]
        )

    def tile_rows(a0):
        return pl.ds(pl.multiple_of(COPIES * a0, 64), COPIES * chunk)

    def shape(weights, signals):
        shaped = []
        for i in range(3):
            rows = slice(8 * i, 8 * i + 8)
            shaped.append(sum(weights[3 * i + j] * signals[j][:, rows] for j in range(3)))
        return shaped

    def pick(ref, k):
        return ref[pl.ds(k, BLOCKS, stride=COPIES), :]

    def to_lines(blocks, base):
        both = jnp.concatenate(blocks, axis=1)
        high, low = split(both)
        mid = dot(first_ref[...], jnp.concatenate([high, low, high], axis=0))
        out = []
        for j in range(2):
            real = mid[:LINES, ROWS * j : ROWS * (j + 1)]
            imag = mid[LINES:, ROWS * j : ROWS * (j + 1)]
            out.append(jnp.concatenate([real * cosine + imag * sine, imag * cosine - real * sine], axis=1))
        keep(jnp.concatenate(out, axis=0), base)

    def keep(values, base):
        high, low = split(values)
        spec_high[base : base + 2 * LINES, :] = high
        spec_low[base : base + 2 * LINES, :] = low

    def over_rows(begin, count):
        rows = slice(LINES * begin, LINES * (begin + count))
        high = spec_high[rows, :]
        return dot(jnp.concatenate([high, spec_low[rows, :], high], axis=1), forward_ref[...])

    def from_lines(values):
        pieces = []
        for j in range(2):
            imag = values[LINES * j : LINES * (j + 1), :ROWS]
            real = values[LINES * j : LINES * (j + 1), ROWS:]
            pieces.append(jnp.concatenate([real * cosine - imag * sine, imag * cosine + real * sine], axis=0))
        high, low = split(jnp.concatenate(pieces, axis=1))
        both = dot(last_ref[...], jnp.concatenate([high, low, high], axis=0))
        return both[:, :ROWS], both[:, ROWS:]

    def spin(values, amount):
        return pltpu.roll(values, amount, values.ndim - 1) if amount else values

    def shape_steps(gi):
        weights = own_weights[gi]
        carry = [jnp.zeros((24, ROWS), f32)] * 2
        mix, grad, ones, twos, forms = (ref.at[gi % 2] for ref in (left, right, shift_one, shift_two, formed))

        def step(a0):
            if a0 == 0:
                arriving(gi).wait()
            raw = raw_buf[gi, a0 : a0 + chunk].astype(f32)
            signal = raw[:, :24]
            one = pltpu.roll(signal, 1, 2)
            two = pltpu.roll(signal, 2, 2)
            one_before = jnp.concatenate([carry[0][None], one[:-1]], axis=0)
            two_before = jnp.concatenate([carry[1][None], two[:-1]], axis=0)
            delayed = (jnp.where(lane < 1, one_before, one), jnp.where(lane < 2, two_before, two))
            ones[a0 : a0 + chunk] = delayed[0]
            twos[a0 : a0 + chunk] = delayed[1]
            shaped = shape(weights, (signal,) + delayed)
            forms[a0 : a0 + chunk] = jnp.concatenate(shaped, axis=1)
            rows = slice(COPIES * a0, COPIES * (a0 + chunk))
            mix[rows, :] = (shaped[1] * shaped[2]).reshape(COPIES * chunk, ROWS)
            grad[rows, :] = (raw[:, 24:] * shaped[0]).reshape(COPIES * chunk, ROWS)
            carry[:] = [one[-1], two[-1]]

        return [functools.partial(step, a0) for a0 in range(0, BLOCKS, chunk)]

    def finish_steps(gi):
        weights = own_weights[gi]
        sums = [jnp.zeros((COPIES, ROWS), f32)] * 10
        mix, grad, ones, twos, forms = (ref.at[gi % 2] for ref in (left, right, shift_one, shift_two, formed))

        def step(a0):
            rows = slice(COPIES * a0, COPIES * (a0 + chunk))
            raw = raw_buf[gi, a0 : a0 + chunk].astype(f32)
            upstream = raw[:, 24:]
            signals = (raw[:, :24], ones[a0 : a0 + chunk], twos[a0 : a0 + chunk])
            shaped = [forms[a0 : a0 + chunk, 8 * i : 8 * i + 8] for i in range(3)]
            mixer = shaped[1] * shaped[2]
            grad_conv = upstream * shaped[0]
            conv = mix[rows, :].reshape(chunk, COPIES, ROWS) + weights[9] * mixer
            grad_mixer = grad[rows, :].reshape(chunk, COPIES, ROWS) + weights[9] * grad_conv
            grads = (upstream * conv, grad_mixer * shaped[2], grad_mixer * shaped[1])
            for i in range(3):
                for j in range(3):
                    sums[3 * i + j] += jnp.sum(grads[i] * signals[j][:, 8 * i : 8 * i + 8], axis=0)
            sums[9] += jnp.sum(grad_conv * mixer, axis=0)

            codes = []
            entry = jnp.zeros((COPIES, ROWS), f32)
            for slot, value in ((0, conv), (1, grad_mixer)):
                scale = scale_of(jnp.max(jnp.max(jnp.abs(value), axis=0), axis=1, keepdims=True))
                codes.append(encode(value, scale).astype(bf16))
                entry = entry + jnp.where(flat == 32 * gi + SCALE + slot, scale, 0.0)
            code_buf[gi, a0 : a0 + chunk] = jnp.concatenate(codes, axis=1)
            ahead = jnp.zeros((chunk, COPIES, ROWS), f32)
            behind = jnp.broadcast_to(entry, (chunk, COPIES, ROWS))
            for i in range(3):
                place = 32 * gi + AFTER + 2 * i
                ahead = jnp.where((lane >= place) & (lane < place + 2), spin(grads[i], place), ahead)
                place = 32 * gi + BEFORE + 2 * i
                moved = spin(signals[2][:, 8 * i : 8 * i + 8], place)
                behind = jnp.where((lane >= place) & (lane < place + 2), moved, behind)
            here = slice(a0, a0 + chunk)
            extra[here] = ahead if gi == 0 else extra[here] + ahead
            exact[here] = behind if gi == 0 else exact[here] + behind
            if a0 + chunk == BLOCKS:
                leaving(gi).start()
                total = jnp.zeros((COPIES, ROWS), f32)
                for i in range(10):
                    value = jnp.sum(sums[i], axis=1, keepdims=True) * (1.0 / math.sqrt(BLOCKS * ROWS))
                    total = total + jnp.where(flat == 32 * gi + TOTAL + i, value, 0.0)
                totals[gi] = total

        return [functools.partial(step, a0) for a0 in range(0, BLOCKS, chunk)]

    def take(steps):
        if steps:
            steps.pop(0)()

    def main(gi, before, after):
        mix, grad = left.at[gi % 2], right.at[gi % 2]
        for base, ref in ((0, mix), (COPIES, grad)):
            for k in range(0, COPIES, GANG):
                for j in range(k, k + GANG, 2):
                    to_lines([pick(ref, j), pick(ref, j + 1)], LINES * (base + j))
                    take(before)
                lines[LINES * (base + k) : LINES * (base + k + GANG), :] = over_rows(base + k, GANG)

        filt_real, filt_imag = filt[gi, :, :ROWS], filt[gi, :, ROWS:]
        cross_real = jnp.zeros((LINES, ROWS), f32)
        cross_imag = jnp.zeros((LINES, ROWS), f32)
        for pair in range(COPIES // 2):
            forth, back = [], []
            for k in (2 * pair, 2 * pair + 1):
                here = slice(LINES * k, LINES * (k + 1))
                there = slice(LINES * (COPIES + k), LINES * (COPIES + k + 1))
                mix_real, mix_imag = lines[here, :ROWS], lines[here, ROWS:]
                grad_real, grad_imag = lines[there, :ROWS], lines[there, ROWS:]
                forth.append(
                    jnp.concatenate(
                        [mix_real * filt_imag + mix_imag * filt_real, mix_real * filt_real - mix_imag * filt_imag], axis=1
                    )
                )
                back.append(
                    jnp.concatenate(
                        [
                            grad_imag * filt_real - grad_real * filt_imag,
                            grad_real * filt_real + grad_imag * filt_imag,
                        ],
                        axis=1,
                    )
                )
                cross_real = cross_real + grad_real * mix_real + grad_imag * mix_imag
                cross_imag = cross_imag + grad_imag * mix_real - grad_real * mix_imag
            keep(jnp.concatenate(forth, axis=0), 2 * LINES * pair)
            keep(jnp.concatenate(back, axis=0), 2 * LINES * (COPIES // 2 + pair))
        cross[gi] = jnp.concatenate([cross_imag, cross_real], axis=1)
        for k in range(0, COPIES, GANG):
            for target, base in ((mix, 0), (grad, COPIES)):
                values = over_rows(base + k, GANG)
                for j in range(0, GANG, 2):
                    pair = from_lines(values[LINES * j : LINES * (j + 2), :])
                    for i in range(2):
                        target[pl.ds(k + j + i, BLOCKS, stride=COPIES), :] = pair[i]
                    take(after)

    def filter_gradient():
        for f in range(0, OWN, 2):
            keep(cross[f : f + 2].reshape(2 * LINES, 2 * ROWS), LINES * f)
        temporal = over_rows(0, OWN)
        scale = 1.0 / math.sqrt(BLOCKS * ROWS * 2 * COPIES)
        values = []
        for f in range(0, OWN, 2):
            values.extend(from_lines(temporal[LINES * f : LINES * (f + 2)]))
        codes = []
        scales = jnp.zeros((BLOCKS, ROWS), f32)
        for f in range(OWN):
            value = values[f] * scale
            size = scale_of(jnp.max(jnp.abs(value), axis=1, keepdims=True))
            codes.append(encode(value, size))
            scales = jnp.where(flat == 32 * f + FILTER_SCALE, size, scales)
        for k in range(COPIES):
            moved = jnp.zeros((BLOCKS, ROWS), f32)
            for f in range(OWN):
                inside = (flat >= 32 * f + SPLIT) & (flat < 32 * f + 32)
                moved = jnp.where(inside, spin(codes[f], (32 * f + SPLIT - 16 * k) % ROWS), moved)
            own[pl.ds(k, BLOCKS, stride=COPIES), :] = moved
            own_scale[pl.ds(k, BLOCKS, stride=COPIES), :] = scales

    def wrap_up():
        every = totals[0] + totals[1] + totals[2] + totals[3]

        def write(step, _):
            a0 = chunk * step
            value = extra[pl.ds(a0 + 1, chunk)] + every[None]
            high = value.astype(bf16).astype(f32)
            code = own[tile_rows(a0), :].reshape(chunk, COPIES, ROWS)
            single = exact[pl.ds(a0, chunk)] + own_scale[tile_rows(a0), :].reshape(chunk, COPIES, ROWS)
            both = [jnp.where(lane % 32 < SPLIT, high, code), jnp.where(lane % 32 < SPLIT, value - high, single)]
            code_buf[OWN, pl.ds(a0, chunk)] = jnp.concatenate(both, axis=1).astype(bf16)
            return 0

        lax.fori_loop(0, steps, write, 0, unroll=8)

    def widen(a, _):
        taps[pl.ds(pl.multiple_of(2 * OWN * a, 2 * OWN), 2 * OWN), :] = taps_ref[a].astype(f32)
        return 0

    lax.fori_loop(0, BLOCKS, widen, 0, unroll=8)
    blocks = []
    for f in range(OWN):
        parts = [taps[pl.ds(OWN * part + f, BLOCKS, stride=2 * OWN), :] for part in range(2)]
        blocks.append(parts[0] + parts[1])
    for f in range(0, OWN, 2):
        to_lines(blocks[f : f + 2], LINES * f)
    filt[...] = over_rows(0, OWN).reshape(OWN, LINES, 2 * ROWS)
    extra[BLOCKS] = jnp.zeros((COPIES, ROWS), f32)
    for step in shape_steps(0):
        step()
    before = []
    for gi in range(OWN):
        after = shape_steps(gi + 1) if gi + 1 < OWN else []
        main(gi, before, after)
        before = finish_steps(gi)
    filter_gradient()
    for step in before:
        step()
    wrap_up()
    leaving(OWN).start()
    for gi in range(OWN + 1):
        leaving(gi).wait()


def extras_kernel(in_ref, spread_ref, mine_ref, other_ref, ext_ref, wide):
    half = lax.axis_index("ch")

    def widen(d, _):
        wide[pl.ds(pl.multiple_of(16 * d, 16), 16), :] = in_ref[d].astype(f32)
        return 0

    lax.fori_loop(0, BLOCKS, widen, 0, unroll=8)
    turned = [wide[pl.ds(n, BLOCKS, stride=16), :].T.astype(bf16) for n in range(2 * COPIES)]
    total = jnp.zeros((2 * COPIES * 32, GROUPS), f32)
    for gi in range(OWN):
        rows = slice(32 * gi, 32 * gi + 32)
        total = total + dot(jnp.concatenate([piece[rows] for piece in turned], axis=0), spread_ref[gi])
    for k in range(COPIES):
        first = total[32 * k : 32 * k + 32]
        second = total[32 * (COPIES + k) : 32 * (COPIES + k) + 32]
        value = decode(first[SPLIT:], second[FILTER_SCALE : FILTER_SCALE + 1])
        low, high = value[:, : GROUPS // 2], value[:, GROUPS // 2 :]
        mine_ref[16 * k : 16 * (k + 1), :] = jnp.where(half == 0, low, high)
        other_ref[16 * k : 16 * (k + 1), :] = jnp.where(half == 0, high, low)
        ext_ref[k, :SPLIT, :] = first[:SPLIT] + second[:SPLIT]
        ext_ref[k, SPLIT:, :] = second[SPLIT:]


def prepare_kernel(feat_ref, weight_ref, out_ref):
    row = lax.broadcasted_iota(jnp.int32, (ROWS, 1), 0)
    for i in range(3):
        value = feat_ref[i].astype(f32)
        one = jnp.where(row < 1, 0.0, pltpu.roll(value, 1, 0))
        two = jnp.where(row < 2, 0.0, pltpu.roll(value, 2, 0))
        out_ref[i] = weight_ref[i, 0:1, :] * value + weight_ref[i, 1:2, :] * one + weight_ref[i, 2:3, :] * two


def finish_kernel(
    in_ref, shaped_ref, cot_ref, weight_ref, ext_ref, mixed_ref, grad_ref, short_ref, skip_ref,
    mixed, grad, wide, turned, mixed_sem, grad_sem,
):
    def lanes_of(k):
        return pl.ds(pl.multiple_of(GROUPS * k, GROUPS), GROUPS)

    def wide_lanes(k):
        return pl.ds(pl.multiple_of(2 * GROUPS * k, 2 * GROUPS), 2 * GROUPS)

    def results(k):
        return (
            pltpu.make_async_copy(mixed.at[k], mixed_ref.at[:, wide_lanes(k)], mixed_sem.at[k]),
            pltpu.make_async_copy(grad.at[k], grad_ref.at[:, :, wide_lanes(k)], grad_sem.at[k]),
        )

    def widen(d, _):
        place = pl.ds(pl.multiple_of(RESULT_ROWS * d, RESULT_ROWS), RESULT_ROWS)
        wide[place, :] = in_ref[d, :RESULT_ROWS, :].astype(f32)
        return 0

    lax.fori_loop(0, BLOCKS, widen, 0, unroll=8)

    size = 16
    row = lax.broadcasted_iota(jnp.int32, (size, 1), 0)

    def one(k0, _):
        for part in range(2):
            half(k0, part)
        for copy in results(k0):
            copy.start()
        return 0

    def half(k0, part):
        k = 2 * k0 + part
        lanes = lanes_of(k)
        spot = slice(GROUPS * part, GROUPS * (part + 1))
        for i in range(3):
            short_ref[i, :, lanes] = ext_ref[k, TOTAL + 3 * i : TOTAL + 3 * i + 3, :]
        skip_ref[:, lanes] = ext_ref[k, TOTAL + 9 : TOTAL + 10, :]
        scales = [ext_ref[k, SCALE + slot : SCALE + slot + 1, :] for slot in range(2)]
        for slot in range(2):
            turned[slot] = wide[pl.ds(8 * slot + k, GROUPS, stride=16), :].T
        taps = [[weight_ref[i, j : j + 1, lanes] for j in range(3)] for i in range(3)]

        following = [ext_ref[k, AFTER + 2 * i : AFTER + 2 * i + 2, :] for i in range(3)]
        lead = []
        for i in range(3):
            second, final = (ext_ref[k, BEFORE + 2 * i + j : BEFORE + 2 * i + j + 1, :] for j in range(2))
            lead.append((taps[i][1] * final + taps[i][2] * second, taps[i][2] * final))
        for begin in reversed(range(0, ROWS, size)):
            rows = slice(begin, begin + size)
            conv, grad_mixer = (decode(turned[slot, rows, :], scales[slot]) for slot in range(2))
            forms = [shaped_ref[i, rows, lanes] for i in range(3)]
            if begin == 0:
                for i in range(3):
                    forms[i] = forms[i] + jnp.where(row == 0, lead[i][0], jnp.where(row == 1, lead[i][1], 0.0))
            query, key, value = forms
            mixed[k0, rows, spot] = (query * conv).astype(bf16)
            slopes = (cot_ref[rows, lanes].astype(f32) * conv, grad_mixer * value, grad_mixer * key)
            for i in range(3):
                slope, after = slopes[i], following[i]
                one = jnp.where(row == size - 1, after[0:1], pltpu.roll(slope, size - 1, 0))
                two = jnp.where(row >= size - 2, pltpu.roll(one, size - 1, 0), pltpu.roll(slope, size - 2, 0))
                two = jnp.where(row == size - 1, after[1:2], two)
                grad[k0, i, rows, spot] = taps[i][0] * slope + taps[i][1] * one + taps[i][2] * two
            following = [slope[:2] for slope in slopes]

    lax.fori_loop(0, COPIES // 2, one, 0)
    for k in range(COPIES // 2):
        for copy in results(k):
            copy.wait()


def exchange(values):
    return lax.all_to_all(values, "ctx", split_axis=0, concat_axis=0, tiled=True)


def pack(features, cotangent, long_filter):
    anywhere = pl.BlockSpec(memory_space=pl.ANY)
    return pl.pallas_call(
        pack_kernel,
        in_specs=[anywhere] * 3,
        out_specs=anywhere,
        out_shape=jax.ShapeDtypeStruct((BLOCKS, SEND_ROWS, ROWS), bf16),
        scratch_shapes=[
            pltpu.VMEM((COPIES, 3, ROWS, GROUPS), bf16),
            pltpu.VMEM((COPIES, ROWS, GROUPS), bf16),
            pltpu.VMEM((ROWS, GROUPS), f32),
            pltpu.VMEM((BLOCKS, SEND_ROWS, ROWS), bf16),
            pltpu.VMEM((4, (COPIES + 1) * SPACING, ROWS), f32),
            pltpu.VMEM((2, GROUPS, ROWS), f32),
            pltpu.SemaphoreType.DMA((COPIES,)),
            pltpu.SemaphoreType.DMA((COPIES,)),
            pltpu.SemaphoreType.DMA,
            pltpu.SemaphoreType.DMA((4,)),
        ],
        compiler_params=ROOMY,
        name="pack",
    )(features, cotangent, long_filter)


def convolve(gathered, own):
    constants = tables()
    anywhere = pl.BlockSpec(memory_space=pl.ANY)
    whole = lambda array: pl.BlockSpec(array.shape, lambda i: (0,) * array.ndim)
    return pl.pallas_call(
        conv_kernel,
        grid=(1,),
        in_specs=[
            anywhere,
            pl.BlockSpec((BLOCKS, 2 * OWN, ROWS), lambda i: (0, SIGNAL_ROWS // (2 * OWN), 0)),
            whole(own),
        ]
        + [whole(array) for array in constants],
        out_specs=anywhere,
        out_shape=jax.ShapeDtypeStruct((BLOCKS, BACK_ROWS, ROWS), bf16),
        scratch_shapes=[
            pltpu.VMEM((OWN, BLOCKS, 4 * COPIES, ROWS), bf16),
            pltpu.VMEM((OWN + 1, BLOCKS, 2 * COPIES, ROWS), bf16),
            pltpu.SemaphoreType.DMA((OWN,)),
            pltpu.SemaphoreType.DMA((OWN + 1,)),
            pltpu.VMEM((2, COPIES * (BLOCKS + 1), ROWS), f32),
            pltpu.VMEM((2, COPIES * (BLOCKS + 1), ROWS), f32),
            pltpu.VMEM((2, BLOCKS, 24, ROWS), f32),
            pltpu.VMEM((2, BLOCKS, 24, ROWS), f32),
            pltpu.VMEM((2, BLOCKS, 24, ROWS), f32),
            pltpu.VMEM((2 * COPIES * LINES, 2 * ROWS), bf16),
            pltpu.VMEM((2 * COPIES * LINES, 2 * ROWS), bf16),
            pltpu.VMEM((2 * COPIES * LINES, 2 * ROWS), f32),
            pltpu.VMEM((OWN, LINES, 2 * ROWS), f32),
            pltpu.VMEM((OWN, LINES, 2 * ROWS), f32),
            pltpu.VMEM((BLOCKS + 1, COPIES, ROWS), f32),
            pltpu.VMEM((BLOCKS, COPIES, ROWS), f32),
            pltpu.VMEM((2 * OWN * (BLOCKS + 1), ROWS), f32),
            pltpu.VMEM((OWN, COPIES, ROWS), f32),
            pltpu.VMEM((COPIES * (BLOCKS + 1), ROWS), f32),
            pltpu.VMEM((COPIES * (BLOCKS + 1), ROWS), f32),
        ],
        compiler_params=LIMIT,
        name="conv",
    )(gathered, gathered, own, *constants)


def unpack_extras(home):
    spread = np.zeros((OWN, BLOCKS, GROUPS), ml_dtypes.bfloat16)
    for gi in range(OWN):
        spread[gi, np.arange(BLOCKS), OWN * np.arange(BLOCKS) + gi] = 1.0
    return pl.pallas_call(
        extras_kernel,
        grid=(1,),
        in_specs=[
            pl.BlockSpec((BLOCKS, 2 * COPIES, ROWS), lambda i: (0, RESULT_ROWS // (2 * COPIES), 0)),
            pl.BlockSpec((OWN, BLOCKS, GROUPS), lambda i: (0, 0, 0)),
        ],
        out_specs=[
            pl.BlockSpec((ROWS, GROUPS // 2), lambda i: (0, 0)),
            pl.BlockSpec((ROWS, GROUPS // 2), lambda i: (0, 0)),
            pl.BlockSpec((COPIES, 32, GROUPS), lambda i: (0, 0, 0)),
        ],
        out_shape=[
            jax.ShapeDtypeStruct((ROWS, GROUPS // 2), f32),
            jax.ShapeDtypeStruct((ROWS, GROUPS // 2), f32),
            jax.ShapeDtypeStruct((COPIES, 32, GROUPS), f32),
        ],
        scratch_shapes=[pltpu.VMEM((16 * (BLOCKS + 1), ROWS), f32)],
        compiler_params=LIMIT,
        name="extras",
    )(home, spread)


def prepare(features, short_weight):
    breadth = features.shape[2]
    deep = lambda k: (0, 0, k)
    width = 2 * GROUPS
    return pl.pallas_call(
        prepare_kernel,
        grid=(breadth // width,),
        in_specs=[pl.BlockSpec((3, ROWS, width), deep), pl.BlockSpec((3, 3, width), deep)],
        out_specs=pl.BlockSpec((3, ROWS, width), deep),
        out_shape=jax.ShapeDtypeStruct((3, ROWS, breadth), f32),
        compiler_params=LIMIT,
        name="prepare",
    )(features, short_weight)


def finish(home, shaped, cotangent, short_weight, ext):
    breadth = shaped.shape[2]
    anywhere = pl.BlockSpec(memory_space=pl.ANY)
    vmem = pl.BlockSpec(memory_space=pltpu.VMEM)
    return pl.pallas_call(
        finish_kernel,
        in_specs=[vmem] * 5,
        out_specs=[anywhere, anywhere, vmem, vmem],
        out_shape=[
            jax.ShapeDtypeStruct((ROWS, breadth), bf16),
            jax.ShapeDtypeStruct((3, ROWS, breadth), f32),
            jax.ShapeDtypeStruct((3, 3, breadth), f32),
            jax.ShapeDtypeStruct((1, breadth), f32),
        ],
        scratch_shapes=[
            pltpu.VMEM((COPIES // 2, ROWS, 2 * GROUPS), bf16),
            pltpu.VMEM((COPIES // 2, 3, ROWS, 2 * GROUPS), f32),
            pltpu.VMEM((RESULT_ROWS * BLOCKS + 16, ROWS), f32),
            pltpu.VMEM((2, ROWS, GROUPS), f32),
            pltpu.SemaphoreType.DMA((COPIES,)),
            pltpu.SemaphoreType.DMA((COPIES,)),
        ],
        compiler_params=LIMIT,
        name="finish",
    )(home, shaped, cotangent, short_weight, ext)


def shards(features, short_weight, skip, long_filter, cotangent):
    breadth = features.shape[2]

    gathered = exchange(pack(features, cotangent, long_filter))

    weights = jnp.concatenate([short_weight.reshape(9, breadth), skip[None]], axis=0)
    weights = weights.reshape(10, COPIES, GROUPS)

    shaped = prepare(features, short_weight)

    gathered, weights, shaped = lax.optimization_barrier((gathered, weights, shaped))
    home = exchange(convolve(gathered, weights))

    mine, other, ext = unpack_extras(home)
    arrived = lax.ppermute(other, "ch", [(0, 1), (1, 0)])
    mixed, feature_gradient, grad_short, grad_skip = finish(home, shaped, cotangent, short_weight, ext)
    return (mixed, feature_gradient, grad_short, grad_skip.reshape(breadth), mine + arrived)


def solution(mesh):
    return jax.shard_map(
        shards,
        mesh=mesh,
        in_specs=(
            P(None, "ctx", "ch"),
            P(None, None, "ch"),
            P("ch"),
            P("ctx", None),
            P("ctx", "ch"),
        ),
        out_specs=(
            P("ctx", "ch"),
            P(None, "ctx", "ch"),
            P(None, None, "ch"),
            P("ch"),
            P("ctx", "ch"),
        ),
        check_vma=False,
    )
```
